512 devices in a mesh: seq: 128 (over z_hi, y, x, core), sub: 4 (over z_lo).
Axes of the slice: x: 4, y: 8, z: 8 (z_hi: 2, z_lo: 4; z = z_hi * 4 + z_lo), core: 2. Of those that a mesh axis runs over, the one named last changes fastest.
Arguments:
- tokens: bfloat16 [65536, 2048], P(('seq', 'sub')), may hold values from -6 to 6
- cotangent: bfloat16 [65536, 2048], P(('seq', 'sub')), may hold values from -6 to 6
- query_gain: float32 [3, 2048], replicated, may hold values from -6 to 6
- key_gain: float32 [3, 2048], replicated, may hold values from -6 to 6
Outputs:
- output: bfloat16 [65536, 2048], P(('seq', 'sub'))
- input_grad: bfloat16 [65536, 2048], P(('seq', 'sub'))
The draws below stay inside these ranges and needn't reach their ends.
All inputs are finite; a program needn't handle non-finite values.
Results may differ from the reference program's by a relative error of at most 0.04.
Values may be sent and summed in bfloat16 or wider, within the bound.
A program may use at most 64 MiB of HBM per device.

```python
import jax
import jax.numpy as jnp
from jax import lax

HEADS = 16
ROWS = 128
WIDTH = 2048
WINDOW = 128
TOKENS = 65536


def draw_query_gain(key, part):
    key = jax.random.fold_in(key, 1)
    return jnp.clip(1.2 * jax.random.normal(key, (3, WIDTH)), -6.0, 6.0).astype(jnp.float32)


def draw_key_gain(key, part):
    key = jax.random.fold_in(key, 2)
    return jnp.clip(1.2 * jax.random.normal(key, (3, WIDTH)), -6.0, 6.0).astype(jnp.float32)


def draw_tokens(key, part):
    key = jax.random.fold_in(key, 3)
    base_key = jax.random.fold_in(key, 0)
    return jnp.clip(jax.random.normal(base_key, (TOKENS, WIDTH)), -6.0, 6.0).astype(jnp.bfloat16)


def levels(own_key, dims, pieces, low, largest):
    level, own = 1.0, jax.random.fold_in(own_key, 6)
    for dim, shards_of in pieces:
        draws = jnp.exp(jax.random.uniform(jax.random.fold_in(own, dim), (shards_of,), jnp.float32, low / len(pieces), largest / len(pieces)))
        level = level * jnp.repeat(draws, dims[dim] // shards_of).reshape([-1 if axis == dim else 1 for axis in range(len(dims))])
    return level


def noise(key, extent, spread, limit, shards=(), held_as=jnp.bfloat16):
    array = jax.random.normal(key, extent, jnp.float32) * spread
    if len(shards) > 0:
        array = levels(key, extent, shards, -0.22, 0.18) * array
    return jnp.clip(array, min=-limit, max=limit).astype(held_as)


def setup_inputs(seed: int = 0) -> dict:
    arg_keys = jax.random.split(jax.random.key(seed), 5)
    tokens = draw_tokens(jax.random.fold_in(arg_keys[4], 71), 0)
    cotangent = noise(arg_keys[1], (TOKENS, WIDTH), 1.0, 6.0, ((0, 512),))
    query_gain = draw_query_gain(jax.random.fold_in(arg_keys[4], 71), 0)
    key_gain = draw_key_gain(jax.random.fold_in(arg_keys[4], 71), 0)
    return {"tokens": tokens, "cotangent": cotangent, "query_gain": query_gain, "key_gain": key_gain}


EPSILON = 1e-06
NEGATIVE_FILL = -1e+30

def rounded(values):
    return lax.optimization_barrier(values.astype(jnp.bfloat16)).astype(jnp.float32)

def normalize(rows_per_level):
    widened = rows_per_level.astype(jnp.float32)
    inv_rms = lax.rsqrt(lax.optimization_barrier(jnp.mean(widened * widened, axis=-1, keepdims=True)) + EPSILON)
    return (lax.optimization_barrier((widened * inv_rms).astype(jnp.bfloat16)), inv_rms)

def norm_backward(rows_per_level, inv_rms, grad_normed):
    unit_rows = rows_per_level.astype(jnp.float32) * inv_rms
    return inv_rms * (grad_normed - unit_rows * lax.optimization_barrier(jnp.mean(grad_normed * unit_rows, axis=-1, keepdims=True)))

def window_mask(query_pos, key_pos, window):
    ahead = query_pos[:, None] - key_pos[None, :]
    return (ahead >= 0) & (ahead < window) & (key_pos[None, :] >= 0)

def split_heads(matrix, head_count):
    return matrix.reshape(matrix.shape[0], head_count, matrix.shape[1] // head_count)

def head_probs(query_heads, key_heads, allowed):
    head_size = query_heads.shape[2]
    scores = jnp.einsum('qhd,khd->hqk', query_heads, key_heads) * head_size ** (-0.5)
    scores = jnp.where(allowed[None], scores, NEGATIVE_FILL)
    row_max = lax.optimization_barrier(jnp.max(scores, axis=-1, keepdims=True))
    weights = jnp.exp(scores - row_max)
    return weights / lax.optimization_barrier(jnp.sum(weights, axis=-1, keepdims=True))

def gained(normed, gain):
    return rounded(normed.astype(jnp.float32) * gain)

def attend_rows(normed, candidates, query_gain, key_gain, allowed, head_count):
    query_heads = split_heads(gained(normed, query_gain), head_count)
    key_heads = split_heads(gained(candidates, key_gain), head_count)
    value_heads = split_heads(candidates.astype(jnp.float32), head_count)
    weights = rounded(head_probs(query_heads, key_heads, allowed))
    attended = jnp.einsum('hqk,khd->qhd', weights, value_heads)
    return attended.reshape(normed.shape[0], normed.shape[1])

def attend_back(normed, candidates, query_gain, key_gain, allowed, head_count, grad_out):
    head_size = normed.shape[1] // head_count
    query_heads = split_heads(gained(normed, query_gain), head_count)
    key_heads = split_heads(gained(candidates, key_gain), head_count)
    value_heads = split_heads(candidates.astype(jnp.float32), head_count)
    weights = head_probs(query_heads, key_heads, allowed)
    weights_low = rounded(weights)
    grad_heads = split_heads(rounded(grad_out), head_count)
    d_probs = jnp.einsum('qhd,khd->hqk', grad_heads, value_heads)
    center = lax.optimization_barrier(jnp.sum(weights * d_probs, axis=-1, keepdims=True))
    d_scores = rounded(weights * (d_probs - center) * head_size ** (-0.5))
    d_query = jnp.einsum('hqk,khd->qhd', d_scores, key_heads)
    d_keys = jnp.einsum('hqk,qhd->khd', d_scores, query_heads)
    d_values = jnp.einsum('hqk,qhd->khd', weights_low, grad_heads)
    query_term = d_query.reshape(normed.shape) * query_gain
    key_term = d_keys.reshape(candidates.shape) * key_gain + d_values.reshape(candidates.shape)
    return (query_term, key_term)

def level_setup(rows_per_level, window):
    normed, inv_rms = normalize(rows_per_level)
    padded = jnp.concatenate([jnp.zeros((window, rows_per_level.shape[1]), normed.dtype), normed], axis=0)
    return (normed, inv_rms, padded)

def block_mask(block_start, span, window):
    query_pos = block_start + jnp.arange(span, dtype=jnp.int32)
    key_pos = block_start - window + jnp.arange(window + span, dtype=jnp.int32)
    return window_mask(query_pos, key_pos, window)

def level_forward(rows_per_level, query_gain, key_gain, span, window, head_count):
    total_rows, model_width = rows_per_level.shape
    normed, inv_rms, padded = level_setup(rows_per_level, window)

    def one_block(block_index):
        block_start = block_index * span
        allowed = block_mask(block_start, span, window)
        own_rows = lax.dynamic_slice_in_dim(normed, block_start, span, 0)
        candidates = lax.dynamic_slice_in_dim(padded, block_start, window + span, 0)
        attended = attend_rows(own_rows, candidates, query_gain, key_gain, allowed, head_count)
        inputs_here = lax.dynamic_slice_in_dim(rows_per_level, block_start, span, 0)
        return (inputs_here.astype(jnp.float32) + attended).astype(jnp.bfloat16)
    upper_rows = lax.map(one_block, jnp.arange(total_rows // span, dtype=jnp.int32))
    return lax.optimization_barrier(upper_rows.reshape(total_rows, model_width))

def level_backward(rows_per_level, grad_upper, query_gain, key_gain, span, window, head_count):
    total_rows, model_width = rows_per_level.shape
    normed, inv_rms, padded = level_setup(rows_per_level, window)

    def one_block(carried, block_index):
        block_start = block_index * span
        allowed = block_mask(block_start, span, window)
        own_rows = lax.dynamic_slice_in_dim(normed, block_start, span, 0)
        candidates = lax.dynamic_slice_in_dim(padded, block_start, window + span, 0)
        grad_here = lax.dynamic_slice_in_dim(grad_upper, block_start, span, 0)
        inputs_here = lax.dynamic_slice_in_dim(rows_per_level, block_start, span, 0)
        scale_here = lax.dynamic_slice_in_dim(inv_rms, block_start, span, 0)
        query_term, key_term = attend_back(own_rows, candidates, query_gain, key_gain, allowed, head_count, grad_here)
        grad_normed = query_term + key_term[window:] + carried[window - span:]
        result_rows = grad_here + norm_backward(inputs_here, scale_here, grad_normed)
        shifted = jnp.concatenate([jnp.zeros((span, model_width), jnp.float32), carried[:window - span]], axis=0)
        return (key_term[:window] + shifted, result_rows)
    initial = jnp.zeros((window, model_width), jnp.float32)
    _, result_rows = lax.scan(one_block, initial, jnp.arange(total_rows // span, dtype=jnp.int32), reverse=True)
    return result_rows.reshape(total_rows, model_width)

def pool_rows(rows_per_level):
    model_width = rows_per_level.shape[1]
    pooled = lax.optimization_barrier(jnp.mean(rows_per_level.astype(jnp.float32).reshape(-1, 4, model_width), axis=1))
    return lax.optimization_barrier(pooled.astype(jnp.bfloat16))

def upsample(coarse, fine_count):
    extended = jnp.concatenate([jnp.zeros((1, coarse.shape[1]), coarse.dtype), coarse], axis=0)
    return jnp.repeat(extended, 4, axis=0)[1:1 + fine_count]

def upsample_back(grad_fine):
    model_width = grad_fine.shape[1]
    padded = jnp.concatenate([jnp.zeros((1, model_width), jnp.float32), grad_fine, jnp.zeros((3, model_width), jnp.float32)], axis=0)
    return lax.optimization_barrier(jnp.sum(padded.reshape(-1, 4, model_width), axis=1))[1:]

def reference(tokens, cotangent, query_gain, key_gain):
    upper_zero = level_forward(tokens, query_gain[0], key_gain[0], ROWS, WINDOW, HEADS)
    first_input = pool_rows(upper_zero)
    upper_one = level_forward(first_input, query_gain[1], key_gain[1], ROWS, WINDOW, HEADS)
    second_input = pool_rows(upper_one)
    upper_two = level_forward(second_input, query_gain[2], key_gain[2], ROWS, WINDOW, HEADS)
    middle = (upper_one.astype(jnp.float32) + upsample(upper_two, upper_one.shape[0]).astype(jnp.float32)).astype(jnp.bfloat16)
    middle = lax.optimization_barrier(middle)
    output = (upper_zero.astype(jnp.float32) + upsample(middle, tokens.shape[0]).astype(jnp.float32)).astype(jnp.bfloat16)
    grad_top = cotangent.astype(jnp.float32)
    grad_middle = upsample_back(grad_top)
    grad_two = upsample_back(grad_middle)
    back_two = level_backward(second_input, grad_two, query_gain[2], key_gain[2], ROWS, WINDOW, HEADS)
    grad_one = grad_middle + jnp.repeat(back_two, 4, axis=0) * 0.25
    back_one = level_backward(first_input, grad_one, query_gain[1], key_gain[1], ROWS, WINDOW, HEADS)
    grad_zero = grad_top + jnp.repeat(back_one, 4, axis=0) * 0.25
    back_zero = level_backward(tokens, grad_zero, query_gain[0], key_gain[0], ROWS, WINDOW, HEADS)
    return (output, back_zero.astype(jnp.bfloat16))
```

```python
import jax
import jax.numpy as jnp
from jax import lax
from jax.experimental import pallas as pl
from jax.experimental.pallas import tpu as pltpu
from jax.sharding import PartitionSpec as P

HEADS = 16
EPSILON = 1e-06
NEGATIVE_FILL = -1e30
HEAD = 128
ROWS = 128
WIDTH = HEADS * HEAD
MEMBERS = 4
COLS = WIDTH // MEMBERS
MESH = pl.DeviceIdType.MESH
F32 = jnp.float32
BF16 = jnp.bfloat16


def multiple(value, by):
    return pl.multiple_of(value, by)


def iotas(rows, columns):
    shape = (rows, columns)
    return lax.broadcasted_iota(jnp.int32, shape, 0), lax.broadcasted_iota(jnp.int32, shape, 1)


def ones_where(mask):
    return jnp.where(mask, 1.0, 0.0).astype(BF16)


def dot(a, b):
    return lax.dot_general(a, b, (((1,), (0,)), ((), ())), preferred_element_type=F32)


def dot_t(a, b):
    return lax.dot_general(a, b, (((1,), (1,)), ((), ())), preferred_element_type=F32)


def t_dot(a, b):
    return lax.dot_general(a, b, (((0,), (0,)), ((), ())), preferred_element_type=F32)


def split_dot(ones, x):
    high = x.astype(BF16)
    low = (x - high.astype(F32)).astype(BF16)
    return dot(ones, high) + dot(ones, low)


def own_mask():
    query, key = iotas(ROWS, ROWS)
    return key <= query


def gained(normed, gain):
    return (normed.astype(F32) * gain).astype(BF16)


def head_forward(cur, prev, query_gain, key_gain, prev_bias):
    own = own_mask()
    query = gained(cur, query_gain)
    scale = HEAD ** (-0.5)
    scores = jnp.where(
        own,
        dot_t(query, gained(cur, key_gain)) * scale,
        dot_t(query, gained(prev, key_gain)) * scale + prev_bias,
    )
    weights = jnp.exp(scores - jnp.max(scores, axis=-1, keepdims=True))
    probs = weights / jnp.sum(weights, axis=-1, keepdims=True)
    zero = jnp.zeros_like(probs)
    attended = dot(jnp.where(own, probs, zero).astype(BF16), cur) + dot(
        jnp.where(own, zero, probs).astype(BF16), prev
    )
    return probs, attended


def head_backward(cur, prev, query_gain, key_gain, probs, grad):
    own = own_mask()
    query = gained(cur, query_gain)
    zero = jnp.zeros_like(probs)
    d_probs = jnp.where(own, dot_t(grad, cur), dot_t(grad, prev))
    center = jnp.sum(probs * d_probs, axis=-1, keepdims=True)
    d_scores = probs * (d_probs - center) * HEAD ** (-0.5)
    ds_cur = jnp.where(own, d_scores, zero).astype(BF16)
    ds_prev = jnp.where(own, zero, d_scores).astype(BF16)
    p_cur = jnp.where(own, probs, zero).astype(BF16)
    p_prev = jnp.where(own, zero, probs).astype(BF16)
    d_query = dot(ds_cur, gained(cur, key_gain)) + dot(ds_prev, gained(prev, key_gain))
    term_cur = d_query * query_gain + t_dot(ds_cur, query) * key_gain + t_dot(p_cur, grad)
    term_prev = t_dot(ds_prev, query) * key_gain + t_dot(p_prev, grad)
    return term_cur, term_prev


def fold(x):
    return sum(x[:, HEAD * k : HEAD * (k + 1)] for k in range(COLS // HEAD))


def up_matrix():
    row, col = iotas(ROWS, 48)
    inside = (col < 32) & (row >= 4 * col + 3) & (row <= 4 * col + 6)
    return ones_where(inside | ((col == 32) & (row <= 2)))


def repeat_matrix():
    row, col = iotas(ROWS, 32)
    return ones_where((row >= 4 * col) & (row < 4 * col + 4))


def pool_matrix():
    row, col = iotas(32, ROWS)
    return ones_where((col >= 4 * row) & (col < 4 * row + 4))


def kernel(
    groups, tokens_hbm, cot_hbm, qg, kg, out_hbm, grad_hbm,
    tok, cotx, n0, n0p, u0, p0, inv0, gc0, gp0, gr0, g0, out_v,
    h1r, n1r, n1c, n1p, h1, p1, u1, u1_in, gmr, g2r, gmh, g2h,
    sq, sq_in, n2r, n2c, n2p, gl2, gl2h, c2, gp2, r2c, r2p, dz, dz_in,
    u2x, edge, edge_in, midx, midr, b2, b2r, gl1, gc1, gp1, gr1, g1s, g1r, gl0,
    local_sem, send_sem, recv_sem,
):
    seq = lax.axis_index("seq")
    sub = lax.axis_index("sub")
    devices = groups * MEMBERS
    device = seq * MEMBERS + sub
    in_unit = lax.rem(seq, 4)
    unit_base = seq - in_unit

    def at_seq(s):
        return (lax.rem(s + groups, groups), sub)

    def at_device(d):
        d = lax.rem(d + devices, devices)
        return (lax.div(d, MEMBERS), lax.rem(d, MEMBERS))

    def peer(k):
        return lax.rem(sub + k, MEMBERS)

    used = [0]
    sent = []

    def take(count):
        used[0] += count
        return used[0] - count

    def remote(src, dst, index, target):
        return pltpu.make_async_remote_copy(
            src_ref=src, dst_ref=dst, send_sem=send_sem.at[index], recv_sem=recv_sem.at[index],
            device_id=target, device_id_type=MESH,
        )

    def post(src, dst, target):
        copy = remote(src, dst, take(1), target)
        copy.start()
        sent.append(copy)
        return copy

    def to_members(source, target_ref):
        return [post(source(peer(k)), target_ref, (seq, peer(k))) for k in range(1, MEMBERS)]

    def arrived(copies):
        for copy in copies:
            copy.wait_recv()

    def cols(member):
        return pl.ds(multiple(member * COLS, COLS), COLS)

    def rows(index, count):
        return pl.ds(multiple(index * count, count), count)

    load_tok = pltpu.make_async_copy(tokens_hbm, tok, local_sem.at[0])
    load_cot = pltpu.make_async_copy(cot_hbm, cotx.at[pl.ds(0, ROWS)], local_sem.at[1])
    load_tok.start()
    load_cot.start()
    barrier = pltpu.get_barrier_semaphore()
    partners = [at_device(device + 1), at_device(device - 1)]
    partners += [(seq, peer(k)) for k in range(1, MEMBERS)]
    partners += [at_seq(unit_base + lax.rem(in_unit + k, 4)) for k in range(1, 4)]
    partners += [at_seq(unit_base + 4 + k) for k in range(4)]
    partners += [at_seq(unit_base - 4 + k) for k in range(4)]
    for partner in partners:
        pl.semaphore_signal(barrier, inc=1, device_id=partner, device_id_type=MESH)

    load_tok.wait()

    def normalize_rows(block, _):
        here = pl.ds(multiple(block * 16, 16), 16)
        x = tok[here, :].astype(F32)
        inv = lax.rsqrt(jnp.sum(x * x, axis=-1, keepdims=True) / WIDTH + EPSILON)
        inv0[here, :] = inv
        n0[here, :] = (x * inv).astype(BF16)
        return 0

    lax.fori_loop(0, ROWS // 16, normalize_rows, 0)
    pl.semaphore_wait(barrier, len(partners))

    halo_index = take(4)

    def halo(chunk):
        here = cols(chunk)
        return remote(n0.at[:, here], n0p.at[:, here], halo_index + chunk, at_device(device + 1))

    for chunk in range(4):
        halo(chunk).start()
    load_cot.wait()
    cot_edge = post(
        cotx.at[pl.ds(0, 16)], cotx.at[pl.ds(ROWS, 16)], at_device(device - 1)
    )

    bias0 = jnp.where(device > 0, 0.0, NEGATIVE_FILL).astype(F32)

    def forward_chunk(chunk, _):
        halo(chunk).wait_recv()
        for k in range(4):
            here = pl.ds(multiple(chunk * COLS + k * HEAD, HEAD), HEAD)
            probs, attended = head_forward(
                n0[:, here], n0p[:, here], qg[0:1, here], kg[0:1, here], bias0
            )
            p0[chunk * 4 + k] = probs
            u0[:, here] = (tok[:, here].astype(F32) + attended).astype(BF16)
        h1r[:, cols(chunk)] = (dot(pool_matrix(), u0[:, cols(chunk)]) * 0.25).astype(BF16)
        return 0

    lax.fori_loop(0, 4, forward_chunk, 0)

    h1_rows = h1r[...].astype(F32)
    inv1 = lax.rsqrt(jnp.sum(h1_rows * h1_rows, axis=-1, keepdims=True) / WIDTH + EPSILON)
    n1r[...] = (h1_rows * inv1).astype(BF16)
    n1_copies = to_members(lambda t: n1r.at[:, cols(t)], n1c.at[rows(sub, 32)])
    h1_copies = to_members(lambda t: h1r.at[:, cols(t)], h1.at[rows(sub, 32)])
    n1c[rows(sub, 32), :] = n1r[:, cols(sub)]
    h1[rows(sub, 32), :] = h1r[:, cols(sub)]

    cot_edge.wait_recv()
    row, col = iotas(48, ROWS + 16)
    known = (col < ROWS) | (device < devices - 1)
    first = (row < 32) & (col >= 4 * row + 3) & (col <= 4 * row + 6)
    start = 16 * (row - 32) + 15
    second = (row >= 32) & (row < 40) & (col >= start) & (col < start + 16)
    gather = ones_where(known & (first | second))
    for chunk in range(4):
        here = pl.ds(chunk * COLS, COLS)
        summed = dot(gather, cotx[:, here])
        gmr[:, here] = summed[0:32]
        g2r[:, here] = summed[32:40]
    gm_low = u1_in
    gm_low[...] = gmr[...].astype(BF16)

    arrived(n1_copies)
    n1_next = post(n1c, n1p, at_seq(seq + 1))
    g2_copies = to_members(lambda t: g2r.at[:, cols(t)], g2h.at[rows(sub, 8)])
    gm_copies = to_members(lambda t: gm_low.at[:, cols(t)], gmh.at[rows(sub, 32)])
    g2h[rows(sub, 8), :] = g2r[:, cols(sub)]
    gmh[rows(sub, 32), :] = gm_low[:, cols(sub)]

    bias1 = jnp.where(seq > 0, 0.0, NEGATIVE_FILL).astype(F32)

    def gains(level, k):
        here = pl.ds(multiple(sub * COLS + k * HEAD, HEAD), HEAD)
        return qg[level : level + 1, here], kg[level : level + 1, here]

    n1_next.wait_recv()
    arrived(h1_copies)
    for k in range(4):
        here = pl.ds(k * HEAD, HEAD)
        probs, attended = head_forward(n1c[:, here], n1p[:, here], *gains(1, k), bias1)
        p1[k] = probs
        u1[:, here] = (h1[:, here].astype(F32) + attended).astype(BF16)
    h2 = (dot(pool_matrix(), u1[...]) * 0.25).astype(BF16).astype(F32)
    sq[...] = fold(h2 * h2)
    sq_copies = [post(sq, sq_in.at[k - 1], (seq, peer(k))) for k in range(1, MEMBERS)]

    def seq_peer(k):
        return lax.rem(in_unit + k, 4)

    arrived(g2_copies)
    gl2[...] = g2h[...].astype(BF16)

    def head_cols(k):
        return pl.ds(multiple(k * HEAD, HEAD), HEAD)

    gl2_copies = [
        post(gl2.at[:, head_cols(seq_peer(k))], gl2h.at[rows(in_unit, 32)], at_seq(unit_base + seq_peer(k)))
        for k in range(1, 4)
    ]
    gl2h[rows(in_unit, 32), :] = gl2[:, head_cols(in_unit)]

    arrived(sq_copies)
    total = jnp.sum(sq[...] + sq_in[0] + sq_in[1] + sq_in[2], axis=-1, keepdims=True)
    inv2 = lax.rsqrt(total / WIDTH + EPSILON)
    n2r[...] = (h2 * inv2).astype(BF16)
    n2_copies = [
        post(n2r.at[:, head_cols(seq_peer(k))], n2c.at[rows(in_unit, 32)], at_seq(unit_base + seq_peer(k)))
        for k in range(1, 4)
    ]
    n2_copies += [
        post(n2r.at[:, head_cols(seq_peer(k))], n2p.at[rows(in_unit, 32)], at_seq(unit_base + 4 + seq_peer(k)))
        for k in range(4)
    ]
    n2c[rows(in_unit, 32), :] = n2r[:, head_cols(in_unit)]

    arrived(gl2_copies)
    arrived(n2_copies)
    bias2 = jnp.where(unit_base > 0, 0.0, NEGATIVE_FILL).astype(F32)
    gains2 = gains(2, in_unit)
    probs2, attended2 = head_forward(n2c[...], n2p[...], *gains2, bias2)
    term_cur, term_prev = head_backward(n2c[...], n2p[...], *gains2, probs2, gl2h[...])
    c2[:, 0:HEAD] = attended2.astype(BF16)
    c2[:, HEAD : 2 * HEAD] = term_cur.astype(BF16)
    gp2[...] = term_prev.astype(BF16)
    c2_copies = [
        post(gp2.at[rows(seq_peer(k), 32)], r2p.at[in_unit], at_seq(unit_base - 4 + seq_peer(k)))
        for k in range(4)
    ]
    c2_copies += [
        post(c2.at[rows(seq_peer(k), 32)], r2c.at[in_unit], at_seq(unit_base + seq_peer(k)))
        for k in range(1, 4)
    ]
    r2c[in_unit] = c2[rows(in_unit, 32), :]

    arrived(c2_copies)
    unit2 = h2 * inv2
    term2 = jnp.concatenate(
        [r2c[k][:, HEAD : 2 * HEAD].astype(F32) + r2p[k].astype(F32) for k in range(4)], axis=1
    )
    dz[...] = fold(term2 * unit2)
    dz_copies = [post(dz, dz_in.at[k - 1], (seq, peer(k))) for k in range(1, MEMBERS)]
    attended2_rows = jnp.concatenate([r2c[k][:, 0:HEAD].astype(F32) for k in range(4)], axis=1)
    u2 = (h2 + attended2_rows).astype(BF16)
    u2x[0:32, :] = u2
    last2 = u2.astype(F32)[31:32]
    last1 = u1[ROWS - 16 :, :].astype(F32)[15:16] + last2
    row, _ = iotas(16, COLS)
    edge[...] = jnp.where(row == 0, last2, jnp.where(row == 1, last1, 0.0)).astype(BF16)
    edge_copy = post(edge, edge_in, at_seq(seq + 1))

    arrived(dz_copies)
    total = jnp.sum(dz[...] + dz_in[0] + dz_in[1] + dz_in[2], axis=-1, keepdims=True)
    back2 = g2h[...] + inv2 * (term2 - unit2 * (total / WIDTH))
    b2[...] = back2
    b2_copies = to_members(lambda t: b2.at[rows(t, 8)], b2r.at[:, cols(sub)])
    b2r[:, cols(sub)] = b2[rows(sub, 8), :]

    arrived(gm_copies)
    grad1 = gmh[...].astype(F32) + split_dot(repeat_matrix(), b2[...]) * 0.25
    gl1[...] = grad1.astype(BF16)
    back_copies = []
    for k in range(4):
        here = pl.ds(k * HEAD, HEAD)
        term_cur, term_prev = head_backward(
            n1c[:, here], n1p[:, here], *gains(1, k), p1[k], gl1[:, here]
        )
        gp1[k] = term_prev.astype(BF16)
        back_copies.append(post(gp1.at[k], gr1.at[k], at_seq(seq - 1)))
        gc1[:, here] = term_cur

    edge_copy.wait_recv()
    before = jnp.where(seq > 0, edge_in[...].astype(F32), 0.0)
    u2x[32:48, :] = before.astype(BF16)
    up = up_matrix()
    mid = (u1[...].astype(F32) + dot(up, u2x[...])).astype(BF16)
    mid_wide = mid.astype(F32)
    for j in range(MEMBERS):
        midx[j, 0:32, :] = mid[32 * j : 32 * (j + 1)]
        ahead = mid_wide[32 * j - 1 : 32 * j] if j > 0 else before[1:2]
        midx[j, 32:48, :] = jnp.broadcast_to(ahead, (16, COLS)).astype(BF16)

    for k in range(4):
        here = pl.ds(k * HEAD, HEAD)
        back_copies[k].wait_recv()
        g1s[:, here] = (gc1[:, here] + gr1[k].astype(F32)).astype(BF16)
    g1_copies = to_members(lambda t: g1s.at[rows(t, 32)], g1r.at[:, cols(sub)])
    mid_copies = to_members(lambda t: midx.at[t], midr.at[:, cols(sub)])
    g1r[:, cols(sub)] = g1s[rows(sub, 32), :]
    midr[:, cols(sub)] = midx[sub]

    arrived(b2_copies)
    repeat8 = repeat_matrix()[0:32, 0:8]
    arrived(g1_copies)
    unit1 = h1_rows * inv1
    term1 = g1r[...].astype(F32)
    along = jnp.sum(term1 * unit1, axis=-1, keepdims=True) / WIDTH
    back1 = gmr[...] + split_dot(repeat8, b2r[...]) * 0.25 + inv1 * (term1 - unit1 * along)
    gmr[...] = back1

    back_index = take(4)

    def back_halo(chunk):
        here = cols(chunk)
        return remote(gp0.at[:, here], gr0.at[:, here], back_index + chunk, at_device(device - 1))

    def backward_chunk(chunk, _):
        wide = cols(chunk)
        grad = cotx[0:ROWS, wide].astype(F32) + split_dot(repeat_matrix(), gmr[:, wide]) * 0.25
        g0[:, wide] = grad
        gl0[...] = grad.astype(BF16)
        for k in range(4):
            here = pl.ds(multiple(chunk * COLS + k * HEAD, HEAD), HEAD)
            term_cur, term_prev = head_backward(
                n0[:, here], n0p[:, here], qg[0:1, here], kg[0:1, here],
                p0[chunk * 4 + k], gl0[:, k * HEAD : (k + 1) * HEAD],
            )
            gp0[:, here] = term_prev.astype(BF16)
            gc0[:, here] = term_cur
        back_halo(chunk).start()
        return 0

    lax.fori_loop(0, 4, backward_chunk, 0)

    arrived(mid_copies)

    def output_chunk(chunk, _):
        here = cols(chunk)
        out_v[:, here] = (u0[:, here].astype(F32) + dot(up_matrix(), midr[:, here])).astype(BF16)
        return 0

    lax.fori_loop(0, 4, output_chunk, 0)
    store_out = pltpu.make_async_copy(out_v, out_hbm, local_sem.at[2])
    store_out.start()

    for chunk in range(4):
        back_halo(chunk).wait_recv()

    def finish_rows(block, _):
        here = pl.ds(multiple(block * 16, 16), 16)
        inv = inv0[here, :]
        unit = tok[here, :].astype(F32) * inv
        term = gc0[here, :] + gr0[here, :].astype(F32)
        along = jnp.sum(term * unit, axis=-1, keepdims=True) / WIDTH
        u0[here, :] = (g0[here, :] + inv * (term - unit * along)).astype(BF16)
        return 0

    lax.fori_loop(0, ROWS // 16, finish_rows, 0)
    store_grad = pltpu.make_async_copy(u0, grad_hbm, local_sem.at[3])
    store_grad.start()
    for copy in sent:
        copy.wait_send()
    for chunk in range(4):
        halo(chunk).wait_send()
        back_halo(chunk).wait_send()
    store_out.wait()
    store_grad.wait()


def per_device(tokens, cotangent, query_gain, key_gain):
    groups = lax.axis_size("seq")
    shape = jax.ShapeDtypeStruct(tokens.shape, BF16)

    def low(*extent):
        return pltpu.VMEM(extent, BF16)

    def wide(*extent):
        return pltpu.VMEM(extent, F32)

    rows_low = low(ROWS, WIDTH)
    scratch = dict(
        tok=rows_low, cotx=low(ROWS + 16, WIDTH), n0=rows_low, n0p=rows_low, u0=rows_low,
        p0=wide(HEADS, ROWS, ROWS), inv0=wide(ROWS, 1), gc0=wide(ROWS, WIDTH), gp0=rows_low,
        gr0=rows_low, g0=wide(ROWS, WIDTH), out_v=rows_low,
        h1r=low(32, WIDTH), n1r=low(32, WIDTH), n1c=low(ROWS, COLS), n1p=low(ROWS, COLS),
        h1=low(ROWS, COLS), p1=wide(4, ROWS, ROWS), u1=low(ROWS, COLS), u1_in=low(32, WIDTH),
        gmr=wide(32, WIDTH), g2r=wide(8, WIDTH), gmh=low(ROWS, COLS), g2h=wide(32, COLS),
        sq=wide(32, HEAD), sq_in=wide(3, 32, HEAD), n2r=low(32, COLS), n2c=low(ROWS, HEAD),
        n2p=low(ROWS, HEAD), gl2=low(32, COLS), gl2h=low(ROWS, HEAD), c2=low(ROWS, 2 * HEAD),
        gp2=low(ROWS, HEAD), r2c=low(4, 32, 2 * HEAD), r2p=low(4, 32, HEAD), dz=wide(32, HEAD),
        dz_in=wide(3, 32, HEAD), u2x=low(48, COLS), edge=low(16, COLS), edge_in=low(16, COLS),
        midx=low(4, 48, COLS), midr=low(48, WIDTH), b2=wide(32, COLS), b2r=wide(8, WIDTH),
        gl1=low(ROWS, COLS), gc1=wide(ROWS, COLS), gp1=low(4, ROWS, HEAD), gr1=low(4, ROWS, HEAD),
        g1s=low(ROWS, COLS), g1r=low(32, WIDTH), gl0=low(ROWS, COLS),
    )
    hbm = pl.BlockSpec(memory_space=pl.ANY)
    vmem = pl.BlockSpec(memory_space=pltpu.VMEM)

    def body(*refs):
        kernel(groups, *refs)

    return pl.pallas_call(
        body,
        out_shape=(shape, shape),
        in_specs=[hbm, hbm, vmem, vmem],
        out_specs=(hbm, hbm),
        scratch_shapes=list(scratch.values())
        + [
            pltpu.SemaphoreType.DMA((4,)),
            pltpu.SemaphoreType.DMA((72,)),
            pltpu.SemaphoreType.DMA((72,)),
        ],
        compiler_params=pltpu.CompilerParams(
            collective_id=0, has_side_effects=True, vmem_limit_bytes=48 * 2**20
        ),
    )(tokens, cotangent, query_gain, key_gain)


def solution(mesh):
    placed = (P(("seq", "sub"), None), P(("seq", "sub"), None), P(), P())
    return jax.shard_map(
        per_device,
        mesh=mesh,
        in_specs=placed,
        out_specs=(P(("seq", "sub"), None), P(("seq", "sub"), None)),
        check_vma=False,
    )
```

```python
import jax
import jax.numpy as jnp
from jax import lax
from jax.experimental import pallas as pl
from jax.experimental.pallas import tpu as pltpu
from jax.sharding import PartitionSpec as P

HEADS = 16
EPSILON = 1e-06
NEGATIVE_FILL = -1e30
HEAD = 128
ROWS = 128
WIDTH = HEADS * HEAD
MEMBERS = 4
COLS = WIDTH // MEMBERS
MESH = pl.DeviceIdType.MESH
F32 = jnp.float32
BF16 = jnp.bfloat16


def multiple(value, by):
    return pl.multiple_of(value, by)


def iotas(rows, columns):
    shape = (rows, columns)
    return lax.broadcasted_iota(jnp.int32, shape, 0), lax.broadcasted_iota(jnp.int32, shape, 1)


def ones_where(mask):
    return jnp.where(mask, 1.0, 0.0).astype(BF16)


def dot(a, b):
    return lax.dot_general(a, b, (((1,), (0,)), ((), ())), preferred_element_type=F32)


def dot_t(a, b):
    return lax.dot_general(a, b, (((1,), (1,)), ((), ())), preferred_element_type=F32)


def t_dot(a, b):
    return lax.dot_general(a, b, (((0,), (0,)), ((), ())), preferred_element_type=F32)


def split_dot(ones, x):
    high = x.astype(BF16)
    low = (x - high.astype(F32)).astype(BF16)
    return dot(ones, high) + dot(ones, low)


def own_mask():
    query, key = iotas(ROWS, ROWS)
    return key <= query


def gained(normed, gain):
    return (normed.astype(F32) * gain).astype(BF16)


def forward_heads(heads, prev_bias):
    own = own_mask()
    scale = HEAD ** (-0.5)
    queries = [gained(cur, qg) for cur, _, qg, _ in heads]
    near = [dot_t(q, gained(h[0], h[3])) for q, h in zip(queries, heads)]
    far = [dot_t(q, gained(h[1], h[3])) for q, h in zip(queries, heads)]
    scores = [jnp.where(own, a * scale, b * scale + prev_bias) for a, b in zip(near, far)]
    tops = [jnp.max(s, axis=-1, keepdims=True) for s in scores]
    weights = [jnp.exp(s - t) for s, t in zip(scores, tops)]
    sums = [jnp.sum(w, axis=-1, keepdims=True) for w in weights]
    probs = [w / s for w, s in zip(weights, sums)]
    low = [p.astype(BF16) for p in probs]
    zero = jnp.zeros((ROWS, ROWS), BF16)
    attended = [
        dot(jnp.where(own, p, zero), h[0]) + dot(jnp.where(own, zero, p), h[1])
        for p, h in zip(low, heads)
    ]
    return list(zip(probs, attended))


def backward_heads(heads):
    own = own_mask()
    zero = jnp.zeros((ROWS, ROWS), BF16)
    queries = [gained(h[0], h[2]) for h in heads]
    d_probs = [jnp.where(own, dot_t(h[5], h[0]), dot_t(h[5], h[1])) for h in heads]
    low = [h[4].astype(BF16) for h in heads]
    v_cur = [t_dot(jnp.where(own, p, zero), h[5]) for p, h in zip(low, heads)]
    v_prev = [t_dot(jnp.where(own, zero, p), h[5]) for p, h in zip(low, heads)]
    centers = [jnp.sum(h[4] * d, axis=-1, keepdims=True) for h, d in zip(heads, d_probs)]
    d_scores = [
        (h[4] * (d - c) * HEAD ** (-0.5)).astype(BF16) for h, d, c in zip(heads, d_probs, centers)
    ]
    ds_cur = [jnp.where(own, d, zero) for d in d_scores]
    ds_prev = [jnp.where(own, zero, d) for d in d_scores]
    k_prev = [t_dot(d, q) for d, q in zip(ds_prev, queries)]
    k_cur = [t_dot(d, q) for d, q in zip(ds_cur, queries)]
    d_query = [
        dot(a, gained(h[0], h[3])) + dot(b, gained(h[1], h[3]))
        for a, b, h in zip(ds_cur, ds_prev, heads)
    ]
    return [
        (dq * h[2] + kc * h[3] + vc, kp * h[3] + vp)
        for h, dq, kc, vc, kp, vp in zip(heads, d_query, k_cur, v_cur, k_prev, v_prev)
    ]


def packed(column):
    row, col = iotas(32, HEAD)
    line = jnp.sum(jnp.where(row == col, column, 0.0), axis=0, keepdims=True)
    return jnp.broadcast_to(line, (8, HEAD))


def unpacked(tile):
    row, col = iotas(32, HEAD)
    line = jnp.broadcast_to(tile[0:1], (32, HEAD))
    return jnp.sum(jnp.where(row == col, line, 0.0), axis=-1, keepdims=True)


def up_matrix():
    row, col = iotas(ROWS, 48)
    inside = (col < 32) & (row >= 4 * col + 3) & (row <= 4 * col + 6)
    return ones_where(inside | ((col == 32) & (row <= 2)))


def repeat_matrix():
    row, col = iotas(ROWS, 32)
    return ones_where((row >= 4 * col) & (row < 4 * col + 4))


def pool_matrix():
    row, col = iotas(32, ROWS)
    return ones_where((col >= 4 * row) & (col < 4 * row + 4))


def kernel(
    groups, tokens_hbm, cot_hbm, qg_hbm, kg_hbm, out_v, grad_out,
    qg, kg, tok, cotx, n0, n0p, u0, p0, inv0, weight0, gc0, gp0, gr0, g0,
    h1r, n1r, n1c, n1p, h1, p1, u1, gm_low, gmr, g2r, gmh, g2h,
    sq, sq_in, n2r, n2c, n2p, gl2, gl2h, c2, gp2, r2c, r2p, dz, dz_in,
    u1r, u2s, u2r, mid, edge, edge_in, b2, b2r, gl1, gc1, gp1, gr1, g1s, g1r,
    local_sem, send_sem, recv_sem,
):
    seq = lax.axis_index("seq")
    sub = lax.axis_index("sub")
    devices = groups * MEMBERS
    device = seq * MEMBERS + sub
    in_unit = lax.rem(seq, 4)
    unit_base = seq - in_unit

    def at_seq(s):
        return (lax.rem(s + groups, groups), sub)

    def at_device(d):
        d = lax.rem(d + devices, devices)
        return (lax.div(d, MEMBERS), lax.rem(d, MEMBERS))

    def peer(k):
        return lax.rem(sub + k, MEMBERS)

    used = [0]
    sent = []

    def take(count):
        used[0] += count
        return used[0] - count

    def remote(src, dst, index, target):
        return pltpu.make_async_remote_copy(
            src_ref=src, dst_ref=dst, send_sem=send_sem.at[index], recv_sem=recv_sem.at[index],
            device_id=target, device_id_type=MESH,
        )

    def post(src, dst, target):
        copy = remote(src, dst, take(1), target)
        copy.start()
        sent.append(copy)
        return copy

    def to_members(source, target_ref):
        return [post(source(peer(k)), target_ref, (seq, peer(k))) for k in range(1, MEMBERS)]

    def arrived(copies):
        for copy in copies:
            copy.wait_recv()

    def cols(member):
        return pl.ds(multiple(member * COLS, COLS), COLS)

    def rows(index, count):
        return pl.ds(multiple(index * count, count), count)

    load_tok = pltpu.make_async_copy(tokens_hbm, tok, local_sem.at[0])
    load_cot = pltpu.make_async_copy(cot_hbm, cotx.at[pl.ds(0, ROWS)], local_sem.at[1])
    load_qg = pltpu.make_async_copy(qg_hbm, qg, local_sem.at[2])
    load_kg = pltpu.make_async_copy(kg_hbm, kg, local_sem.at[3])
    load_tok.start()
    load_qg.start()
    load_kg.start()
    load_cot.start()
    barrier = pltpu.get_barrier_semaphore()
    partners = [at_device(device + 1), at_device(device - 1)]
    partners += [(seq, peer(k)) for k in range(1, MEMBERS)]
    partners += [at_seq(unit_base + lax.rem(in_unit + k, 4)) for k in range(1, 4)]
    partners += [at_seq(unit_base + 4 + k) for k in range(4)]
    partners += [at_seq(unit_base - 4 + k) for k in range(4)]
    for partner in partners:
        pl.semaphore_signal(barrier, inc=1, device_id=partner, device_id_type=MESH)

    load_tok.wait()

    def normalize_rows(block, _):
        here = pl.ds(multiple(block * 16, 16), 16)
        x = tok[here, :].astype(F32)
        inv = lax.rsqrt(jnp.sum(x * x, axis=-1, keepdims=True) / WIDTH + EPSILON)
        inv0[here, :] = inv
        n0[here, :] = (x * inv).astype(BF16)
        return 0

    lax.fori_loop(0, ROWS // 16, normalize_rows, 0)
    pl.semaphore_wait(barrier, len(partners))

    halo_index = take(4)

    def halo(chunk):
        here = cols(chunk)
        return remote(n0.at[:, here], n0p.at[:, here], halo_index + chunk, at_device(device + 1))

    for chunk in range(4):
        halo(chunk).start()
    load_cot.wait()
    cot_edge = post(
        cotx.at[pl.ds(0, 16)], cotx.at[pl.ds(ROWS, 16)], at_device(device - 1)
    )

    load_qg.wait()
    load_kg.wait()
    bias0 = jnp.where(device > 0, 0.0, NEGATIVE_FILL).astype(F32)

    def forward_chunk(chunk, _):
        halo(chunk).wait_recv()
        spans = [pl.ds(multiple(chunk * COLS + k * HEAD, HEAD), HEAD) for k in range(4)]
        results = forward_heads(
            [(n0[:, here], n0p[:, here], qg[0:1, here], kg[0:1, here]) for here in spans], bias0
        )
        for k, (probs, attended) in enumerate(results):
            p0[chunk * 4 + k] = probs
            u0[:, spans[k]] = (tok[:, spans[k]].astype(F32) + attended).astype(BF16)
        h1r[:, cols(chunk)] = (dot(pool_matrix(), u0[:, cols(chunk)]) * 0.25).astype(BF16)
        return 0

    lax.fori_loop(0, 4, forward_chunk, 0)

    h1_rows = h1r[...].astype(F32)
    inv1 = lax.rsqrt(jnp.sum(h1_rows * h1_rows, axis=-1, keepdims=True) / WIDTH + EPSILON)
    n1r[...] = (h1_rows * inv1).astype(BF16)
    n1_copies = to_members(lambda t: n1r.at[:, cols(t)], n1c.at[rows(sub, 32)])
    h1_copies = to_members(lambda t: h1r.at[:, cols(t)], h1.at[rows(sub, 32)])
    n1c[rows(sub, 32), :] = n1r[:, cols(sub)]
    h1[rows(sub, 32), :] = h1r[:, cols(sub)]

    cot_edge.wait_recv()
    row, col = iotas(48, ROWS + 16)
    known = (col < ROWS) | (device < devices - 1)
    first = (row < 32) & (col >= 4 * row + 3) & (col <= 4 * row + 6)
    start = 16 * (row - 32) + 15
    second = (row >= 32) & (row < 40) & (col >= start) & (col < start + 16)
    gather = ones_where(known & (first | second))
    for chunk in range(4):
        here = pl.ds(chunk * COLS, COLS)
        summed = dot(gather, cotx[:, here])
        gmr[:, here] = summed[0:32]
        g2r[:, here] = summed[32:40]
    gm_low[...] = gmr[...].astype(BF16)

    arrived(n1_copies)
    n1_next = post(n1c, n1p, at_seq(seq + 1))
    g2_copies = to_members(lambda t: g2r.at[:, cols(t)], g2h.at[rows(sub, 8)])
    gm_copies = to_members(lambda t: gm_low.at[:, cols(t)], gmh.at[rows(sub, 32)])
    g2h[rows(sub, 8), :] = g2r[:, cols(sub)]
    gmh[rows(sub, 32), :] = gm_low[:, cols(sub)]

    bias1 = jnp.where(seq > 0, 0.0, NEGATIVE_FILL).astype(F32)

    def gains(level, k):
        here = pl.ds(multiple(sub * COLS + k * HEAD, HEAD), HEAD)
        return qg[level : level + 1, here], kg[level : level + 1, here]

    n1_next.wait_recv()
    spans = [pl.ds(k * HEAD, HEAD) for k in range(4)]
    results = forward_heads(
        [(n1c[:, here], n1p[:, here], *gains(1, k)) for k, here in enumerate(spans)], bias1
    )
    arrived(h1_copies)
    for k, (probs, attended) in enumerate(results):
        p1[k] = probs
        u1[:, spans[k]] = (h1[:, spans[k]].astype(F32) + attended).astype(BF16)
    h2 = (dot(pool_matrix(), u1[...]) * 0.25).astype(BF16).astype(F32)
    sq[...] = packed(jnp.sum(h2 * h2, axis=-1, keepdims=True))
    sq_copies = [post(sq, sq_in.at[k - 1], (seq, peer(k))) for k in range(1, MEMBERS)]

    def seq_peer(k):
        return lax.rem(in_unit + k, 4)

    arrived(g2_copies)
    gl2[...] = g2h[...].astype(BF16)

    def head_cols(k):
        return pl.ds(multiple(k * HEAD, HEAD), HEAD)

    gl2_copies = [
        post(gl2.at[:, head_cols(seq_peer(k))], gl2h.at[rows(in_unit, 32)], at_seq(unit_base + seq_peer(k)))
        for k in range(1, 4)
    ]
    gl2h[rows(in_unit, 32), :] = gl2[:, head_cols(in_unit)]

    arrived(sq_copies)
    total = unpacked(sq[...] + sq_in[0] + sq_in[1] + sq_in[2])
    inv2 = lax.rsqrt(total / WIDTH + EPSILON)
    n2r[...] = (h2 * inv2).astype(BF16)
    n2_copies = [
        post(n2r.at[:, head_cols(seq_peer(k))], n2c.at[rows(in_unit, 32)], at_seq(unit_base + seq_peer(k)))
        for k in range(1, 4)
    ]
    n2_copies += [
        post(n2r.at[:, head_cols(seq_peer(k))], n2p.at[rows(in_unit, 32)], at_seq(unit_base + 4 + seq_peer(k)))
        for k in range(4)
    ]
    n2c[rows(in_unit, 32), :] = n2r[:, head_cols(in_unit)]

    u1_copies = to_members(lambda t: u1.at[rows(t, 32)], u1r.at[:, cols(sub)])
    u1r[:, cols(sub)] = u1[rows(sub, 32), :]

    arrived(gl2_copies)
    arrived(n2_copies)
    bias2 = jnp.where(unit_base > 0, 0.0, NEGATIVE_FILL).astype(F32)
    gains2 = gains(2, in_unit)
    ((probs2, attended2),) = forward_heads([(n2c[...], n2p[...], *gains2)], bias2)
    ((term_cur, term_prev),) = backward_heads([(n2c[...], n2p[...], *gains2, probs2, gl2h[...])])
    c2[:, 0:HEAD] = attended2.astype(BF16)
    c2[:, HEAD : 2 * HEAD] = term_cur.astype(BF16)
    gp2[...] = term_prev.astype(BF16)
    c2_copies = [
        post(gp2.at[rows(seq_peer(k), 32)], r2p.at[in_unit], at_seq(unit_base - 4 + seq_peer(k)))
        for k in range(4)
    ]
    c2_copies += [
        post(c2.at[rows(seq_peer(k), 32)], r2c.at[in_unit], at_seq(unit_base + seq_peer(k)))
        for k in range(1, 4)
    ]
    r2c[in_unit] = c2[rows(in_unit, 32), :]

    arrived(c2_copies)
    unit2 = h2 * inv2
    term2 = jnp.concatenate(
        [r2c[k][:, HEAD : 2 * HEAD].astype(F32) + r2p[k].astype(F32) for k in range(4)], axis=1
    )
    dz[...] = packed(jnp.sum(term2 * unit2, axis=-1, keepdims=True))
    dz_copies = [post(dz, dz_in.at[k - 1], (seq, peer(k))) for k in range(1, MEMBERS)]
    attended2_rows = jnp.concatenate([r2c[k][:, 0:HEAD].astype(F32) for k in range(4)], axis=1)
    u2 = (h2 + attended2_rows).astype(BF16)
    u2_wide = u2.astype(F32)
    row, _ = iotas(16, COLS)

    def u1_row(r):
        return u1[r - 15 : r + 1, :].astype(F32)[15:16]

    edge[...] = jnp.where(
        row == 0, u2_wide[31:32], jnp.where(row == 1, u1_row(ROWS - 1), 0.0)
    ).astype(BF16)
    edge_copy = post(edge, edge_in, at_seq(seq + 1))

    arrived(dz_copies)
    total = unpacked(dz[...] + dz_in[0] + dz_in[1] + dz_in[2])
    back2 = g2h[...] + inv2 * (term2 - unit2 * (total / WIDTH))
    b2[...] = back2
    b2_copies = to_members(lambda t: b2.at[rows(t, 8)], b2r.at[:, cols(sub)])
    b2r[:, cols(sub)] = b2[rows(sub, 8), :]

    arrived(gm_copies)
    grad1 = gmh[...].astype(F32) + split_dot(repeat_matrix(), b2[...]) * 0.25
    gl1[...] = grad1.astype(BF16)
    back_copies = []
    results = backward_heads(
        [
            (n1c[:, here], n1p[:, here], *gains(1, k), p1[k], gl1[:, here])
            for k, here in enumerate(spans)
        ]
    )
    for k, (term_cur, term_prev) in enumerate(results):
        gp1[k] = term_prev.astype(BF16)
        back_copies.append(post(gp1.at[k], gr1.at[k], at_seq(seq - 1)))
        gc1[:, spans[k]] = term_cur

    edge_copy.wait_recv()
    before = edge_in[...].astype(F32)
    row, _ = iotas(8, COLS)
    for t in range(MEMBERS):
        if t == 0:
            coarse, fine = before[0:1], before[1:2]
        else:
            coarse, fine = u2_wide[8 * t - 1 : 8 * t], u1_row(32 * t - 1)
        tail = jnp.where(row == 0, coarse, jnp.where(row == 1, fine, 0.0))
        u2s[t] = jnp.concatenate([u2_wide[8 * t : 8 * t + 8], tail], axis=0).astype(BF16)
    u2_copies = to_members(lambda t: u2s.at[t], u2r.at[:, cols(sub)])
    u2r[:, cols(sub)] = u2s[sub]

    for k in range(4):
        here = pl.ds(k * HEAD, HEAD)
        back_copies[k].wait_recv()
        g1s[:, here] = (gc1[:, here] + gr1[k].astype(F32)).astype(BF16)
    g1_copies = to_members(lambda t: g1s.at[rows(t, 32)], g1r.at[:, cols(sub)])
    g1r[:, cols(sub)] = g1s[rows(sub, 32), :]

    arrived(b2_copies)
    repeat8 = repeat_matrix()[0:32, 0:8]
    arrived(g1_copies)
    unit1 = h1_rows * inv1
    term1 = g1r[...].astype(F32)
    along = jnp.sum(term1 * unit1, axis=-1, keepdims=True) / WIDTH
    back1 = gmr[...] + split_dot(repeat8, b2r[...]) * 0.25 + inv1 * (term1 - unit1 * along)
    gmr[...] = back1

    back_index = take(4)

    def back_halo(chunk):
        here = cols(chunk)
        return remote(gp0.at[:, here], gr0.at[:, here], back_index + chunk, at_device(device - 1))

    def backward_chunk(chunk, _):
        wide = cols(chunk)
        grad = cotx[0:ROWS, wide].astype(F32) + split_dot(repeat_matrix(), gmr[:, wide]) * 0.25
        g0[:, wide] = grad
        spans = [pl.ds(multiple(chunk * COLS + k * HEAD, HEAD), HEAD) for k in range(4)]
        low = grad.astype(BF16)
        results = backward_heads(
            [
                (n0[:, here], n0p[:, here], qg[0:1, here], kg[0:1, here],
                 p0[chunk * 4 + k], low[:, k * HEAD : (k + 1) * HEAD])
                for k, here in enumerate(spans)
            ]
        )
        for here, (_, term_prev) in zip(spans, results):
            gp0[:, here] = term_prev.astype(BF16)
        back_halo(chunk).start()
        for here, (term_cur, _) in zip(spans, results):
            gc0[:, here] = term_cur
        return 0

    lax.fori_loop(0, 4, backward_chunk, 0)

    arrived(u1_copies)
    arrived(u2_copies)
    row, col = iotas(32, 16)
    inside = (col < 8) & (row >= 4 * col + 3) & (row <= 4 * col + 6)
    lift = ones_where(inside | ((col == 8) & (row <= 2) & (device > 0)))

    def output_chunk(chunk, _):
        here = cols(chunk)
        coarse = u2r[:, here]
        mid[0:32, here] = (u1r[:, here].astype(F32) + dot(lift, coarse)).astype(BF16)
        last = coarse.astype(F32)
        last = jnp.where(device > 0, last[8:9] + last[9:10], 0.0)
        mid[32:48, here] = jnp.broadcast_to(last, (16, COLS)).astype(BF16)
        out_v[:, here] = (u0[:, here].astype(F32) + dot(up_matrix(), mid[:, here])).astype(BF16)
        return 0

    lax.fori_loop(0, 4, output_chunk, 0)

    inv = inv0[...]

    def term_chunk(chunk, along):
        here = cols(chunk)
        back_halo(chunk).wait_recv()
        term = gc0[:, here] + gr0[:, here].astype(F32)
        g0[:, here] = g0[:, here] + inv * term
        part = term * tok[:, here].astype(F32)
        return along + sum(part[:, k * HEAD : (k + 1) * HEAD] for k in range(COLS // HEAD))

    along = lax.fori_loop(0, 4, term_chunk, jnp.zeros((ROWS, HEAD), F32))
    weight0[...] = inv * inv * inv * (jnp.sum(along, axis=-1, keepdims=True) / WIDTH)

    def finish_rows(block, _):
        here = pl.ds(multiple(block * 16, 16), 16)
        grad_out[here, :] = (g0[here, :] - weight0[here, :] * tok[here, :].astype(F32)).astype(BF16)
        return 0

    lax.fori_loop(0, ROWS // 16, finish_rows, 0)
    for copy in sent:
        copy.wait_send()
    for chunk in range(4):
        halo(chunk).wait_send()
        back_halo(chunk).wait_send()


def per_device(tokens, cotangent, query_gain, key_gain):
    groups = lax.axis_size("seq")
    shape = jax.ShapeDtypeStruct(tokens.shape, BF16)

    def low(*extent):
        return pltpu.VMEM(extent, BF16)

    def wide(*extent):
        return pltpu.VMEM(extent, F32)

    rows_low = low(ROWS, WIDTH)
    scratch = dict(
        qg=wide(3, WIDTH), kg=wide(3, WIDTH), tok=rows_low, cotx=low(ROWS + 16, WIDTH), n0=rows_low, n0p=rows_low, u0=rows_low,
        p0=wide(HEADS, ROWS, ROWS), inv0=wide(ROWS, 1), weight0=wide(ROWS, 1), gc0=wide(ROWS, WIDTH), gp0=rows_low,
        gr0=rows_low, g0=wide(ROWS, WIDTH),
        h1r=low(32, WIDTH), n1r=low(32, WIDTH), n1c=low(ROWS, COLS), n1p=low(ROWS, COLS),
        h1=low(ROWS, COLS), p1=wide(4, ROWS, ROWS), u1=low(ROWS, COLS), gm_low=low(32, WIDTH),
        gmr=wide(32, WIDTH), g2r=wide(8, WIDTH), gmh=low(ROWS, COLS), g2h=wide(32, COLS),
        sq=wide(8, HEAD), sq_in=wide(3, 8, HEAD), n2r=low(32, COLS), n2c=low(ROWS, HEAD),
        n2p=low(ROWS, HEAD), gl2=low(32, COLS), gl2h=low(ROWS, HEAD), c2=low(ROWS, 2 * HEAD),
        gp2=low(ROWS, HEAD), r2c=low(4, 32, 2 * HEAD), r2p=low(4, 32, HEAD), dz=wide(8, HEAD),
        dz_in=wide(3, 8, HEAD), u1r=low(32, WIDTH), u2s=low(4, 16, COLS), u2r=low(16, WIDTH), mid=low(48, WIDTH), edge=low(16, COLS), edge_in=low(16, COLS),
        b2=wide(32, COLS), b2r=wide(8, WIDTH),
        gl1=low(ROWS, COLS), gc1=wide(ROWS, COLS), gp1=low(4, ROWS, HEAD), gr1=low(4, ROWS, HEAD),
        g1s=low(ROWS, COLS), g1r=low(32, WIDTH),
    )
    hbm = pl.BlockSpec(memory_space=pl.ANY)

    vmem = pl.BlockSpec(memory_space=pltpu.VMEM)

    def body(*refs):
        kernel(groups, *refs)

    return pl.pallas_call(
        body,
        out_shape=(shape, shape),
        in_specs=[hbm] * 4,
        out_specs=(vmem, vmem),
        scratch_shapes=list(scratch.values())
        + [
            pltpu.SemaphoreType.DMA((4,)),
            pltpu.SemaphoreType.DMA((72,)),
            pltpu.SemaphoreType.DMA((72,)),
        ],
        compiler_params=pltpu.CompilerParams(
            collective_id=0, has_side_effects=True, vmem_limit_bytes=int(52.5 * 2**20)
        ),
    )(tokens, cotangent, query_gain, key_gain)


def solution(mesh):
    placed = (P(("seq", "sub"), None), P(("seq", "sub"), None), P(), P())
    return jax.shard_map(
        per_device,
        mesh=mesh,
        in_specs=placed,
        out_specs=(P(("seq", "sub"), None), P(("seq", "sub"), None)),
        check_vma=False,
    )
```

```python
import jax
import jax.numpy as jnp
from jax import lax
from jax.experimental import pallas as pl
from jax.experimental.pallas import tpu as pltpu
from jax.sharding import PartitionSpec as P

HEADS = 16
EPSILON = 1e-06
NEGATIVE_FILL = -1e30
HEAD = 128
ROWS = 128
WIDTH = HEADS * HEAD
MEMBERS = 4
COLS = WIDTH // MEMBERS
MESH = pl.DeviceIdType.MESH
F32 = jnp.float32
BF16 = jnp.bfloat16


def multiple(value, by):
    return pl.multiple_of(value, by)


def iotas(rows, columns):
    shape = (rows, columns)
    return lax.broadcasted_iota(jnp.int32, shape, 0), lax.broadcasted_iota(jnp.int32, shape, 1)


def ones_where(mask):
    return jnp.where(mask, 1.0, 0.0).astype(BF16)


def dot(a, b):
    return lax.dot_general(a, b, (((1,), (0,)), ((), ())), preferred_element_type=F32)


def dot_t(a, b):
    return lax.dot_general(a, b, (((1,), (1,)), ((), ())), preferred_element_type=F32)


def t_dot(a, b):
    return lax.dot_general(a, b, (((0,), (0,)), ((), ())), preferred_element_type=F32)


def split_dot(ones, x):
    high = x.astype(BF16)
    low = (x - high.astype(F32)).astype(BF16)
    return dot(ones, high) + dot(ones, low)


def own_mask():
    query, key = iotas(ROWS, ROWS)
    return key <= query


def gained(normed, gain):
    return (normed.astype(F32) * gain).astype(BF16)


def forward_heads(heads, prev_bias):
    own = own_mask()
    scale = HEAD ** (-0.5)
    queries = [gained(cur, qg) for cur, _, qg, _ in heads]
    near = [dot_t(q, gained(h[0], h[3])) for q, h in zip(queries, heads)]
    far = [dot_t(q, gained(h[1], h[3])) for q, h in zip(queries, heads)]
    scores = [jnp.where(own, a * scale, b * scale + prev_bias) for a, b in zip(near, far)]
    tops = [jnp.max(s, axis=-1, keepdims=True) for s in scores]
    weights = [jnp.exp(s - t) for s, t in zip(scores, tops)]
    sums = [jnp.sum(w, axis=-1, keepdims=True) for w in weights]
    probs = [w / s for w, s in zip(weights, sums)]
    low = [p.astype(BF16) for p in probs]
    zero = jnp.zeros((ROWS, ROWS), BF16)
    attended = [
        dot(jnp.where(own, p, zero), h[0]) + dot(jnp.where(own, zero, p), h[1])
        for p, h in zip(low, heads)
    ]
    return list(zip(probs, attended))


def backward_heads(heads):
    own = own_mask()
    zero = jnp.zeros((ROWS, ROWS), BF16)
    queries = [gained(h[0], h[2]) for h in heads]
    d_probs = [jnp.where(own, dot_t(h[5], h[0]), dot_t(h[5], h[1])) for h in heads]
    low = [h[4].astype(BF16) for h in heads]
    v_cur = [t_dot(jnp.where(own, p, zero), h[5]) for p, h in zip(low, heads)]
    v_prev = [t_dot(jnp.where(own, zero, p), h[5]) for p, h in zip(low, heads)]
    centers = [jnp.sum(h[4] * d, axis=-1, keepdims=True) for h, d in zip(heads, d_probs)]
    d_scores = [
        (h[4] * (d - c) * HEAD ** (-0.5)).astype(BF16) for h, d, c in zip(heads, d_probs, centers)
    ]
    ds_cur = [jnp.where(own, d, zero) for d in d_scores]
    ds_prev = [jnp.where(own, zero, d) for d in d_scores]
    k_prev = [t_dot(d, q) for d, q in zip(ds_prev, queries)]
    k_cur = [t_dot(d, q) for d, q in zip(ds_cur, queries)]
    d_query = [
        dot(a, gained(h[0], h[3])) + dot(b, gained(h[1], h[3]))
        for a, b, h in zip(ds_cur, ds_prev, heads)
    ]
    return [
        (dq * h[2] + kc * h[3] + vc, kp * h[3] + vp)
        for h, dq, kc, vc, kp, vp in zip(heads, d_query, k_cur, v_cur, k_prev, v_prev)
    ]


def packed(column):
    row, col = iotas(32, HEAD)
    line = jnp.sum(jnp.where(row == col, column, 0.0), axis=0, keepdims=True)
    return jnp.broadcast_to(line, (8, HEAD))


def unpacked(tile):
    row, col = iotas(32, HEAD)
    line = jnp.broadcast_to(tile[0:1], (32, HEAD))
    return jnp.sum(jnp.where(row == col, line, 0.0), axis=-1, keepdims=True)


def up_matrix():
    row, col = iotas(ROWS, 48)
    inside = (col < 32) & (row >= 4 * col + 3) & (row <= 4 * col + 6)
    return ones_where(inside | ((col == 32) & (row <= 2)))


def repeat_matrix():
    row, col = iotas(ROWS, 32)
    return ones_where((row >= 4 * col) & (row < 4 * col + 4))


def pool_matrix():
    row, col = iotas(32, ROWS)
    return ones_where((col >= 4 * row) & (col < 4 * row + 4))


class Guarded:
    def __init__(self, copy, sends, takes, blank=None):
        self.copy, self.sends, self.takes, self.blank = copy, sends, takes, blank

    def start(self):
        @pl.when(self.sends)
        def _():
            self.copy.start()

    def wait_recv(self):
        @pl.when(self.takes)
        def _():
            self.copy.wait_recv()

        if self.blank is not None:

            @pl.when(jnp.logical_not(self.takes))
            def _():
                self.blank[...] = jnp.zeros(self.blank.shape, self.blank.dtype)

    def wait_send(self):
        @pl.when(self.sends)
        def _():
            self.copy.wait_send()


def kernel(
    groups, tokens_hbm, cot_hbm, qg_hbm, kg_hbm, out_v, grad_out,
    qg, kg, tok, cotx, n0, n0p, u0, p0, inv0, weight0, gc0, gp0, gr0, g0,
    h1r, n1r, n1c, n1p, h1, p1, u1, gm_low, gmr, g2r, gmh, g2h,
    sq, sq_in, n2r, n2c, n2p, gl2, gl2h, c2, gp2, r2c, r2p, dz, dz_in,
    u1r, u2s, u2r, mid, edge, edge_in, b2, b2r, gl1, gc1, gp1, gr1, g1s, g1r,
    local_sem, send_sem, recv_sem,
):
    seq = lax.axis_index("seq")
    sub = lax.axis_index("sub")
    devices = groups * MEMBERS
    device = seq * MEMBERS + sub
    in_unit = lax.rem(seq, 4)
    unit_base = seq - in_unit

    first_device, last_device = device == 0, device == devices - 1
    first_group, last_group = seq == 0, seq == groups - 1
    first_unit, last_unit = unit_base == 0, unit_base == groups - 4
    no = jnp.logical_not

    def at_seq(s):
        return (lax.rem(s + groups, groups), sub)

    def at_device(d):
        d = lax.rem(d + devices, devices)
        return (lax.div(d, MEMBERS), lax.rem(d, MEMBERS))

    def peer(k):
        return lax.rem(sub + k, MEMBERS)

    used = [0]
    sent = []

    def take(count):
        used[0] += count
        return used[0] - count

    def remote(src, dst, index, target):
        return pltpu.make_async_remote_copy(
            src_ref=src, dst_ref=dst, send_sem=send_sem.at[index], recv_sem=recv_sem.at[index],
            device_id=target, device_id_type=MESH,
        )

    def post(src, dst, target):
        copy = remote(src, dst, take(1), target)
        copy.start()
        sent.append(copy)
        return copy

    def post_if(src, dst, target, sends, takes, blank=None):
        copy = Guarded(remote(src, dst, take(1), target), sends, takes, blank)
        copy.start()
        sent.append(copy)
        return copy

    def to_members(source, target_ref):
        return [post(source(peer(k)), target_ref, (seq, peer(k))) for k in range(1, MEMBERS)]

    def arrived(copies):
        for copy in copies:
            copy.wait_recv()

    def cols(member):
        return pl.ds(multiple(member * COLS, COLS), COLS)

    def rows(index, count):
        return pl.ds(multiple(index * count, count), count)

    load_tok = pltpu.make_async_copy(tokens_hbm, tok, local_sem.at[0])
    load_cot = pltpu.make_async_copy(cot_hbm, cotx.at[pl.ds(0, ROWS)], local_sem.at[1])
    load_qg = pltpu.make_async_copy(qg_hbm, qg, local_sem.at[2])
    load_kg = pltpu.make_async_copy(kg_hbm, kg, local_sem.at[3])
    load_tok.start()
    load_qg.start()
    load_kg.start()
    load_cot.start()
    barrier = pltpu.get_barrier_semaphore()
    partners = [(at_device(device + 1), no(last_device)), (at_device(device - 1), no(first_device))]
    partners += [((seq, peer(k)), None) for k in range(1, MEMBERS)]
    partners += [(at_seq(unit_base + lax.rem(in_unit + k, 4)), None) for k in range(1, 4)]
    partners += [(at_seq(unit_base + 4 + k), no(last_unit)) for k in range(4)]
    partners += [(at_seq(unit_base - 4 + k), no(first_unit)) for k in range(4)]
    expected = 0
    for partner, present in partners:

        def greet(partner=partner):
            pl.semaphore_signal(barrier, inc=1, device_id=partner, device_id_type=MESH)

        if present is None:
            greet()
            expected = expected + 1
        else:
            pl.when(present)(greet)
            expected = expected + jnp.where(present, 1, 0)

    load_tok.wait()

    def normalize_rows(block, _):
        here = pl.ds(multiple(block * 16, 16), 16)
        x = tok[here, :].astype(F32)
        inv = lax.rsqrt(jnp.sum(x * x, axis=-1, keepdims=True) / WIDTH + EPSILON)
        inv0[here, :] = inv
        n0[here, :] = (x * inv).astype(BF16)
        return 0

    lax.fori_loop(0, ROWS // 16, normalize_rows, 0)
    pl.semaphore_wait(barrier, expected)

    halo_index = take(4)

    def halo(chunk):
        here = cols(chunk)
        copy = remote(n0.at[:, here], n0p.at[:, here], halo_index + chunk, at_device(device + 1))
        return Guarded(copy, no(last_device), no(first_device), n0p.at[:, here])

    for chunk in range(4):
        halo(chunk).start()
    load_cot.wait()
    cot_edge = post_if(
        cotx.at[pl.ds(0, 16)], cotx.at[pl.ds(ROWS, 16)], at_device(device - 1),
        no(first_device), no(last_device), cotx.at[pl.ds(ROWS, 16)],
    )

    load_qg.wait()
    load_kg.wait()
    bias0 = jnp.where(device > 0, 0.0, NEGATIVE_FILL).astype(F32)

    def forward_chunk(chunk, _):
        halo(chunk).wait_recv()
        spans = [pl.ds(multiple(chunk * COLS + k * HEAD, HEAD), HEAD) for k in range(4)]
        results = forward_heads(
            [(n0[:, here], n0p[:, here], qg[0:1, here], kg[0:1, here]) for here in spans], bias0
        )
        for k, (probs, attended) in enumerate(results):
            p0[chunk * 4 + k] = probs
            u0[:, spans[k]] = (tok[:, spans[k]].astype(F32) + attended).astype(BF16)
        h1r[:, cols(chunk)] = (dot(pool_matrix(), u0[:, cols(chunk)]) * 0.25).astype(BF16)
        return 0

    lax.fori_loop(0, 4, forward_chunk, 0)

    h1_rows = h1r[...].astype(F32)
    inv1 = lax.rsqrt(jnp.sum(h1_rows * h1_rows, axis=-1, keepdims=True) / WIDTH + EPSILON)
    n1r[...] = (h1_rows * inv1).astype(BF16)
    n1_copies = to_members(lambda t: n1r.at[:, cols(t)], n1c.at[rows(sub, 32)])
    h1_copies = to_members(lambda t: h1r.at[:, cols(t)], h1.at[rows(sub, 32)])
    n1c[rows(sub, 32), :] = n1r[:, cols(sub)]
    h1[rows(sub, 32), :] = h1r[:, cols(sub)]

    cot_edge.wait_recv()
    row, col = iotas(48, ROWS + 16)
    first = (row < 32) & (col >= 4 * row + 3) & (col <= 4 * row + 6)
    start = 16 * (row - 32) + 15
    second = (row >= 32) & (row < 40) & (col >= start) & (col < start + 16)
    gather = ones_where(first | second)
    for chunk in range(4):
        here = pl.ds(chunk * COLS, COLS)
        summed = dot(gather, cotx[:, here])
        gmr[:, here] = summed[0:32]
        g2r[:, here] = summed[32:40]
    gm_low[...] = gmr[...].astype(BF16)

    arrived(n1_copies)
    n1_next = post_if(n1c, n1p, at_seq(seq + 1), no(last_group), no(first_group), n1p)
    g2_copies = to_members(lambda t: g2r.at[:, cols(t)], g2h.at[rows(sub, 8)])
    gm_copies = to_members(lambda t: gm_low.at[:, cols(t)], gmh.at[rows(sub, 32)])
    g2h[rows(sub, 8), :] = g2r[:, cols(sub)]
    gmh[rows(sub, 32), :] = gm_low[:, cols(sub)]

    bias1 = jnp.where(seq > 0, 0.0, NEGATIVE_FILL).astype(F32)

    def gains(level, k):
        here = pl.ds(multiple(sub * COLS + k * HEAD, HEAD), HEAD)
        return qg[level : level + 1, here], kg[level : level + 1, here]

    n1_next.wait_recv()
    spans = [pl.ds(k * HEAD, HEAD) for k in range(4)]
    results = forward_heads(
        [(n1c[:, here], n1p[:, here], *gains(1, k)) for k, here in enumerate(spans)], bias1
    )
    arrived(h1_copies)
    for k, (probs, attended) in enumerate(results):
        p1[k] = probs
        u1[:, spans[k]] = (h1[:, spans[k]].astype(F32) + attended).astype(BF16)
    h2 = (dot(pool_matrix(), u1[...]) * 0.25).astype(BF16).astype(F32)
    sq[...] = packed(jnp.sum(h2 * h2, axis=-1, keepdims=True))
    sq_copies = [post(sq, sq_in.at[k - 1], (seq, peer(k))) for k in range(1, MEMBERS)]

    def seq_peer(k):
        return lax.rem(in_unit + k, 4)

    arrived(g2_copies)
    gl2[...] = g2h[...].astype(BF16)

    def head_cols(k):
        return pl.ds(multiple(k * HEAD, HEAD), HEAD)

    gl2_copies = [
        post(gl2.at[:, head_cols(seq_peer(k))], gl2h.at[rows(in_unit, 32)], at_seq(unit_base + seq_peer(k)))
        for k in range(1, 4)
    ]
    gl2h[rows(in_unit, 32), :] = gl2[:, head_cols(in_unit)]

    arrived(sq_copies)
    total = unpacked(sq[...] + sq_in[0] + sq_in[1] + sq_in[2])
    inv2 = lax.rsqrt(total / WIDTH + EPSILON)
    n2r[...] = (h2 * inv2).astype(BF16)
    n2_copies = [
        post(n2r.at[:, head_cols(seq_peer(k))], n2c.at[rows(in_unit, 32)], at_seq(unit_base + seq_peer(k)))
        for k in range(1, 4)
    ]
    n2_copies += [
        post_if(
            n2r.at[:, head_cols(seq_peer(k))], n2p.at[rows(in_unit, 32)],
            at_seq(unit_base + 4 + seq_peer(k)),
            no(last_unit), no(first_unit), n2p if k == 0 else None,
        )
        for k in range(4)
    ]
    n2c[rows(in_unit, 32), :] = n2r[:, head_cols(in_unit)]

    u1_copies = to_members(lambda t: u1.at[rows(t, 32)], u1r.at[:, cols(sub)])
    u1r[:, cols(sub)] = u1[rows(sub, 32), :]

    arrived(gl2_copies)
    arrived(n2_copies)
    bias2 = jnp.where(unit_base > 0, 0.0, NEGATIVE_FILL).astype(F32)
    gains2 = gains(2, in_unit)
    ((probs2, attended2),) = forward_heads([(n2c[...], n2p[...], *gains2)], bias2)
    ((term_cur, term_prev),) = backward_heads([(n2c[...], n2p[...], *gains2, probs2, gl2h[...])])
    c2[:, 0:HEAD] = attended2.astype(BF16)
    c2[:, HEAD : 2 * HEAD] = term_cur.astype(BF16)
    gp2[...] = term_prev.astype(BF16)
    c2_copies = [
        post_if(
            gp2.at[rows(seq_peer(k), 32)], r2p.at[in_unit], at_seq(unit_base - 4 + seq_peer(k)),
            no(first_unit), no(last_unit), r2p if k == 0 else None,
        )
        for k in range(4)
    ]
    c2_copies += [
        post(c2.at[rows(seq_peer(k), 32)], r2c.at[in_unit], at_seq(unit_base + seq_peer(k)))
        for k in range(1, 4)
    ]
    r2c[in_unit] = c2[rows(in_unit, 32), :]

    arrived(c2_copies)
    unit2 = h2 * inv2
    term2 = jnp.concatenate(
        [r2c[k][:, HEAD : 2 * HEAD].astype(F32) + r2p[k].astype(F32) for k in range(4)], axis=1
    )
    dz[...] = packed(jnp.sum(term2 * unit2, axis=-1, keepdims=True))
    dz_copies = [post(dz, dz_in.at[k - 1], (seq, peer(k))) for k in range(1, MEMBERS)]
    attended2_rows = jnp.concatenate([r2c[k][:, 0:HEAD].astype(F32) for k in range(4)], axis=1)
    u2 = (h2 + attended2_rows).astype(BF16)
    u2_wide = u2.astype(F32)
    row, _ = iotas(16, COLS)

    def u1_row(r):
        return u1[r - 15 : r + 1, :].astype(F32)[15:16]

    edge[...] = jnp.where(
        row == 0, u2_wide[31:32], jnp.where(row == 1, u1_row(ROWS - 1), 0.0)
    ).astype(BF16)
    edge_copy = post_if(edge, edge_in, at_seq(seq + 1), no(last_group), no(first_group), edge_in)

    arrived(dz_copies)
    total = unpacked(dz[...] + dz_in[0] + dz_in[1] + dz_in[2])
    back2 = g2h[...] + inv2 * (term2 - unit2 * (total / WIDTH))
    b2[...] = back2
    b2_copies = to_members(lambda t: b2.at[rows(t, 8)], b2r.at[:, cols(sub)])
    b2r[:, cols(sub)] = b2[rows(sub, 8), :]

    arrived(gm_copies)
    grad1 = gmh[...].astype(F32) + split_dot(repeat_matrix(), b2[...]) * 0.25
    gl1[...] = grad1.astype(BF16)
    back_copies = []
    results = backward_heads(
        [
            (n1c[:, here], n1p[:, here], *gains(1, k), p1[k], gl1[:, here])
            for k, here in enumerate(spans)
        ]
    )
    for k, (term_cur, term_prev) in enumerate(results):
        gp1[k] = term_prev.astype(BF16)
        back_copies.append(
            post_if(
                gp1.at[k], gr1.at[k], at_seq(seq - 1), no(first_group), no(last_group), gr1.at[k]
            )
        )
        gc1[:, spans[k]] = term_cur

    edge_copy.wait_recv()
    before = edge_in[...].astype(F32)
    row, _ = iotas(8, COLS)
    for t in range(MEMBERS):
        if t == 0:
            coarse, fine = before[0:1], before[1:2]
        else:
            coarse, fine = u2_wide[8 * t - 1 : 8 * t], u1_row(32 * t - 1)
        tail = jnp.where(row == 0, coarse, jnp.where(row == 1, fine, 0.0))
        u2s[t] = jnp.concatenate([u2_wide[8 * t : 8 * t + 8], tail], axis=0).astype(BF16)
    u2_copies = to_members(lambda t: u2s.at[t], u2r.at[:, cols(sub)])
    u2r[:, cols(sub)] = u2s[sub]

    for k in range(4):
        here = pl.ds(k * HEAD, HEAD)
        back_copies[k].wait_recv()
        g1s[:, here] = (gc1[:, here] + gr1[k].astype(F32)).astype(BF16)
    g1_copies = to_members(lambda t: g1s.at[rows(t, 32)], g1r.at[:, cols(sub)])
    g1r[:, cols(sub)] = g1s[rows(sub, 32), :]

    arrived(b2_copies)
    repeat8 = repeat_matrix()[0:32, 0:8]
    arrived(g1_copies)
    unit1 = h1_rows * inv1
    term1 = g1r[...].astype(F32)
    along = jnp.sum(term1 * unit1, axis=-1, keepdims=True) / WIDTH
    back1 = gmr[...] + split_dot(repeat8, b2r[...]) * 0.25 + inv1 * (term1 - unit1 * along)
    gmr[...] = back1

    back_index = take(4)

    def back_halo(chunk):
        here = cols(chunk)
        copy = remote(gp0.at[:, here], gr0.at[:, here], back_index + chunk, at_device(device - 1))
        return Guarded(copy, no(first_device), no(last_device), gr0.at[:, here])

    def backward_chunk(chunk, _):
        wide = cols(chunk)
        grad = cotx[0:ROWS, wide].astype(F32) + split_dot(repeat_matrix(), gmr[:, wide]) * 0.25
        g0[:, wide] = grad
        spans = [pl.ds(multiple(chunk * COLS + k * HEAD, HEAD), HEAD) for k in range(4)]
        low = grad.astype(BF16)
        results = backward_heads(
            [
                (n0[:, here], n0p[:, here], qg[0:1, here], kg[0:1, here],
                 p0[chunk * 4 + k], low[:, k * HEAD : (k + 1) * HEAD])
                for k, here in enumerate(spans)
            ]
        )
        for here, (_, term_prev) in zip(spans, results):
            gp0[:, here] = term_prev.astype(BF16)
        back_halo(chunk).start()
        for here, (term_cur, _) in zip(spans, results):
            gc0[:, here] = term_cur
        return 0

    lax.fori_loop(0, 4, backward_chunk, 0)

    arrived(u1_copies)
    arrived(u2_copies)
    row, col = iotas(32, 16)
    inside = (col < 8) & (row >= 4 * col + 3) & (row <= 4 * col + 6)
    lift = ones_where(inside | ((col == 8) & (row <= 2) & (device > 0)))

    def output_chunk(chunk, _):
        here = cols(chunk)
        coarse = u2r[:, here]
        mid[0:32, here] = (u1r[:, here].astype(F32) + dot(lift, coarse)).astype(BF16)
        last = coarse.astype(F32)
        last = jnp.where(device > 0, last[8:9] + last[9:10], 0.0)
        mid[32:48, here] = jnp.broadcast_to(last, (16, COLS)).astype(BF16)
        out_v[:, here] = (u0[:, here].astype(F32) + dot(up_matrix(), mid[:, here])).astype(BF16)
        return 0

    lax.fori_loop(0, 4, output_chunk, 0)

    inv = inv0[...]

    def term_chunk(chunk, along):
        here = cols(chunk)
        back_halo(chunk).wait_recv()
        term = gc0[:, here] + gr0[:, here].astype(F32)
        g0[:, here] = g0[:, here] + inv * term
        part = term * tok[:, here].astype(F32)
        return along + sum(part[:, k * HEAD : (k + 1) * HEAD] for k in range(COLS // HEAD))

    along = lax.fori_loop(0, 4, term_chunk, jnp.zeros((ROWS, HEAD), F32))
    weight0[...] = inv * inv * inv * (jnp.sum(along, axis=-1, keepdims=True) / WIDTH)

    def finish_rows(block, _):
        here = pl.ds(multiple(block * 16, 16), 16)
        grad_out[here, :] = (g0[here, :] - weight0[here, :] * tok[here, :].astype(F32)).astype(BF16)
        return 0

    lax.fori_loop(0, ROWS // 16, finish_rows, 0)
    for copy in sent:
        copy.wait_send()
    for chunk in range(4):
        halo(chunk).wait_send()
        back_halo(chunk).wait_send()


def per_device(tokens, cotangent, query_gain, key_gain):
    groups = lax.axis_size("seq")
    shape = jax.ShapeDtypeStruct(tokens.shape, BF16)

    def low(*extent):
        return pltpu.VMEM(extent, BF16)

    def wide(*extent):
        return pltpu.VMEM(extent, F32)

    rows_low = low(ROWS, WIDTH)
    scratch = dict(
        qg=wide(3, WIDTH), kg=wide(3, WIDTH), tok=rows_low, cotx=low(ROWS + 16, WIDTH), n0=rows_low, n0p=rows_low, u0=rows_low,
        p0=wide(HEADS, ROWS, ROWS), inv0=wide(ROWS, 1), weight0=wide(ROWS, 1), gc0=wide(ROWS, WIDTH), gp0=rows_low,
        gr0=rows_low, g0=wide(ROWS, WIDTH),
        h1r=low(32, WIDTH), n1r=low(32, WIDTH), n1c=low(ROWS, COLS), n1p=low(ROWS, COLS),
        h1=low(ROWS, COLS), p1=wide(4, ROWS, ROWS), u1=low(ROWS, COLS), gm_low=low(32, WIDTH),
        gmr=wide(32, WIDTH), g2r=wide(8, WIDTH), gmh=low(ROWS, COLS), g2h=wide(32, COLS),
        sq=wide(8, HEAD), sq_in=wide(3, 8, HEAD), n2r=low(32, COLS), n2c=low(ROWS, HEAD),
        n2p=low(ROWS, HEAD), gl2=low(32, COLS), gl2h=low(ROWS, HEAD), c2=low(ROWS, 2 * HEAD),
        gp2=low(ROWS, HEAD), r2c=low(4, 32, 2 * HEAD), r2p=low(4, 32, HEAD), dz=wide(8, HEAD),
        dz_in=wide(3, 8, HEAD), u1r=low(32, WIDTH), u2s=low(4, 16, COLS), u2r=low(16, WIDTH), mid=low(48, WIDTH), edge=low(16, COLS), edge_in=low(16, COLS),
        b2=wide(32, COLS), b2r=wide(8, WIDTH),
        gl1=low(ROWS, COLS), gc1=wide(ROWS, COLS), gp1=low(4, ROWS, HEAD), gr1=low(4, ROWS, HEAD),
        g1s=low(ROWS, COLS), g1r=low(32, WIDTH),
    )
    hbm = pl.BlockSpec(memory_space=pl.ANY)

    vmem = pl.BlockSpec(memory_space=pltpu.VMEM)

    def body(*refs):
        kernel(groups, *refs)

    return pl.pallas_call(
        body,
        out_shape=(shape, shape),
        in_specs=[hbm] * 4,
        out_specs=(vmem, vmem),
        scratch_shapes=list(scratch.values())
        + [
            pltpu.SemaphoreType.DMA((4,)),
            pltpu.SemaphoreType.DMA((72,)),
            pltpu.SemaphoreType.DMA((72,)),
        ],
        compiler_params=pltpu.CompilerParams(
            collective_id=0, has_side_effects=True, vmem_limit_bytes=int(52.5 * 2**20)
        ),
    )(tokens, cotangent, query_gain, key_gain)


def solution(mesh):
    placed = (P(("seq", "sub"), None), P(("seq", "sub"), None), P(), P())
    return jax.shard_map(
        per_device,
        mesh=mesh,
        in_specs=placed,
        out_specs=(P(("seq", "sub"), None), P(("seq", "sub"), None)),
        check_vma=False,
    )
```

```python
import jax
import jax.numpy as jnp
from jax import lax
from jax.experimental import pallas as pl
from jax.experimental.pallas import tpu as pltpu
from jax.sharding import PartitionSpec as P

HEADS = 16
EPSILON = 1e-06
NEGATIVE_FILL = -1e30
HEAD = 128
ROWS = 128
WIDTH = HEADS * HEAD
MEMBERS = 4
COLS = WIDTH // MEMBERS
MESH = pl.DeviceIdType.MESH
F32 = jnp.float32
BF16 = jnp.bfloat16


def multiple(value, by):
    return pl.multiple_of(value, by)


def iotas(rows, columns):
    shape = (rows, columns)
    return lax.broadcasted_iota(jnp.int32, shape, 0), lax.broadcasted_iota(jnp.int32, shape, 1)


def ones_where(mask):
    return jnp.where(mask, 1.0, 0.0).astype(BF16)


def dot(a, b):
    return lax.dot_general(a, b, (((1,), (0,)), ((), ())), preferred_element_type=F32)


def dot_t(a, b):
    return lax.dot_general(a, b, (((1,), (1,)), ((), ())), preferred_element_type=F32)


def t_dot(a, b):
    return lax.dot_general(a, b, (((0,), (0,)), ((), ())), preferred_element_type=F32)


def split_dot(ones, x):
    high = x.astype(BF16)
    low = (x - high.astype(F32)).astype(BF16)
    return dot(ones, high) + dot(ones, low)


def own_mask():
    query, key = iotas(ROWS, ROWS)
    return key <= query


def gained(normed, gain):
    return (normed.astype(F32) * gain).astype(BF16)


def forward_heads(heads, prev_bias):
    own = own_mask()
    scale = HEAD ** (-0.5)
    queries = [gained(cur, qg) for cur, _, qg, _ in heads]
    near = [dot_t(q, gained(h[0], h[3])) for q, h in zip(queries, heads)]
    far = [dot_t(q, gained(h[1], h[3])) for q, h in zip(queries, heads)]
    scores = [jnp.where(own, a * scale, b * scale + prev_bias) for a, b in zip(near, far)]
    tops = [jnp.max(s, axis=-1, keepdims=True) for s in scores]
    weights = [jnp.exp(s - t) for s, t in zip(scores, tops)]
    sums = [jnp.sum(w, axis=-1, keepdims=True) for w in weights]
    probs = [w / s for w, s in zip(weights, sums)]
    low = [p.astype(BF16) for p in probs]
    zero = jnp.zeros((ROWS, ROWS), BF16)
    attended = [
        dot(jnp.where(own, p, zero), h[0]) + dot(jnp.where(own, zero, p), h[1])
        for p, h in zip(low, heads)
    ]
    return list(zip(probs, attended))


def backward_heads(heads):
    own = own_mask()
    zero = jnp.zeros((ROWS, ROWS), BF16)
    queries = [gained(h[0], h[2]) for h in heads]
    d_probs = [jnp.where(own, dot_t(h[5], h[0]), dot_t(h[5], h[1])) for h in heads]
    low = [h[4].astype(BF16) for h in heads]
    v_prev = [t_dot(jnp.where(own, zero, p), h[5]) for p, h in zip(low, heads)]
    centers = [jnp.sum(h[4] * d, axis=-1, keepdims=True) for h, d in zip(heads, d_probs)]
    d_scores = [
        (h[4] * (d - c) * HEAD ** (-0.5)).astype(BF16) for h, d, c in zip(heads, d_probs, centers)
    ]
    ds_cur = [jnp.where(own, d, zero) for d in d_scores]
    ds_prev = [jnp.where(own, zero, d) for d in d_scores]
    k_prev = [t_dot(d, q) for d, q in zip(ds_prev, queries)]
    terms_prev = [kp * h[3] + vp for h, kp, vp in zip(heads, k_prev, v_prev)]

    def own_terms():
        v_cur = [t_dot(jnp.where(own, p, zero), h[5]) for p, h in zip(low, heads)]
        k_cur = [t_dot(d, q) for d, q in zip(ds_cur, queries)]
        d_query = [
            dot(a, gained(h[0], h[3])) + dot(b, gained(h[1], h[3]))
            for a, b, h in zip(ds_cur, ds_prev, heads)
        ]
        return [
            dq * h[2] + kc * h[3] + vc for h, dq, kc, vc in zip(heads, d_query, k_cur, v_cur)
        ]

    return terms_prev, own_terms


def packed(column):
    row, col = iotas(32, HEAD)
    line = jnp.sum(jnp.where(row == col, column, 0.0), axis=0, keepdims=True)
    return jnp.broadcast_to(line, (8, HEAD))


def unpacked(tile):
    row, col = iotas(32, HEAD)
    line = jnp.broadcast_to(tile[0:1], (32, HEAD))
    return jnp.sum(jnp.where(row == col, line, 0.0), axis=-1, keepdims=True)


def up_matrix():
    row, col = iotas(ROWS, 48)
    inside = (col < 32) & (row >= 4 * col + 3) & (row <= 4 * col + 6)
    return ones_where(inside | ((col == 32) & (row <= 2)))


def repeat_matrix():
    row, col = iotas(ROWS, 32)
    return ones_where((row >= 4 * col) & (row < 4 * col + 4))


def pool_matrix():
    row, col = iotas(32, ROWS)
    return ones_where((col >= 4 * row) & (col < 4 * row + 4))


class Guarded:
    def __init__(self, copy, sends, takes, blank=None):
        self.copy, self.sends, self.takes, self.blank = copy, sends, takes, blank

    def start(self):
        @pl.when(self.sends)
        def _():
            self.copy.start()

    def wait_recv(self):
        @pl.when(self.takes)
        def _():
            self.copy.wait_recv()

        if self.blank is not None:

            @pl.when(jnp.logical_not(self.takes))
            def _():
                self.blank[...] = jnp.zeros(self.blank.shape, self.blank.dtype)

    def wait_send(self):
        @pl.when(self.sends)
        def _():
            self.copy.wait_send()


def kernel(
    groups, tokens_hbm, cot_hbm, qg_hbm, kg_hbm, out_v, grad_out,
    qg, kg, tok, cotx, n0, n0p, u0, p0, inv0, weight0, gc0, gp0, gr0, g0,
    h1r, n1r, n1c, n1p, h1, p1, u1, gm_low, gmr, g2r, gmh, g2h,
    sq, sq_in, n2r, n2c, n2p, gl2, gl2h, c2, gp2, r2c, r2p, dz, dz_in,
    u1r, u2s, u2r, mid, edge, edge_in, b2, b2r, gl1, gc1, gp1, gr1, g1s, g1r,
    local_sem, send_sem, recv_sem,
):
    seq = lax.axis_index("seq")
    sub = lax.axis_index("sub")
    devices = groups * MEMBERS
    device = seq * MEMBERS + sub
    in_unit = lax.rem(seq, 4)
    unit_base = seq - in_unit

    first_device, last_device = device == 0, device == devices - 1
    first_group, last_group = seq == 0, seq == groups - 1
    first_unit, last_unit = unit_base == 0, unit_base == groups - 4
    no = jnp.logical_not

    def at_seq(s):
        return (lax.rem(s + groups, groups), sub)

    def at_device(d):
        d = lax.rem(d + devices, devices)
        return (lax.div(d, MEMBERS), lax.rem(d, MEMBERS))

    def peer(k):
        return lax.rem(sub + k, MEMBERS)

    used = [0]
    sent = []

    def take(count):
        used[0] += count
        return used[0] - count

    def remote(src, dst, index, target):
        return pltpu.make_async_remote_copy(
            src_ref=src, dst_ref=dst, send_sem=send_sem.at[index], recv_sem=recv_sem.at[index],
            device_id=target, device_id_type=MESH,
        )

    def post(src, dst, target):
        copy = remote(src, dst, take(1), target)
        copy.start()
        sent.append(copy)
        return copy

    def post_if(src, dst, target, sends, takes, blank=None):
        copy = Guarded(remote(src, dst, take(1), target), sends, takes, blank)
        copy.start()
        sent.append(copy)
        return copy

    def to_members(source, target_ref):
        return [post(source(peer(k)), target_ref, (seq, peer(k))) for k in range(1, MEMBERS)]

    def arrived(copies):
        for copy in copies:
            copy.wait_recv()

    def cols(member):
        return pl.ds(multiple(member * COLS, COLS), COLS)

    def rows(index, count):
        return pl.ds(multiple(index * count, count), count)

    load_tok = pltpu.make_async_copy(tokens_hbm, tok, local_sem.at[0])
    load_cot = pltpu.make_async_copy(cot_hbm, cotx.at[pl.ds(0, ROWS)], local_sem.at[1])
    load_qg = pltpu.make_async_copy(qg_hbm, qg, local_sem.at[2])
    load_kg = pltpu.make_async_copy(kg_hbm, kg, local_sem.at[3])
    load_tok.start()
    load_qg.start()
    load_kg.start()
    load_cot.start()
    barrier = pltpu.get_barrier_semaphore()
    partners = [(at_device(device + 1), no(last_device)), (at_device(device - 1), no(first_device))]
    partners += [((seq, peer(k)), None) for k in range(1, MEMBERS)]
    partners += [(at_seq(unit_base + lax.rem(in_unit + k, 4)), None) for k in range(1, 4)]
    partners += [(at_seq(unit_base + 4 + k), no(last_unit)) for k in range(4)]
    partners += [(at_seq(unit_base - 4 + k), no(first_unit)) for k in range(4)]
    expected = 0
    for partner, present in partners:

        def greet(partner=partner):
            pl.semaphore_signal(barrier, inc=1, device_id=partner, device_id_type=MESH)

        if present is None:
            greet()
            expected = expected + 1
        else:
            pl.when(present)(greet)
            expected = expected + jnp.where(present, 1, 0)

    load_tok.wait()

    def normalize_rows(block, _):
        here = pl.ds(multiple(block * 16, 16), 16)
        x = tok[here, :].astype(F32)
        inv = lax.rsqrt(jnp.sum(x * x, axis=-1, keepdims=True) / WIDTH + EPSILON)
        inv0[here, :] = inv
        n0[here, :] = (x * inv).astype(BF16)
        return 0

    lax.fori_loop(0, ROWS // 16, normalize_rows, 0)
    pl.semaphore_wait(barrier, expected)

    halo_index = take(4)

    def halo(chunk):
        here = cols(chunk)
        copy = remote(n0.at[:, here], n0p.at[:, here], halo_index + chunk, at_device(device + 1))
        return Guarded(copy, no(last_device), no(first_device), n0p.at[:, here])

    for chunk in range(4):
        halo(chunk).start()
    load_cot.wait()
    cot_edge = post_if(
        cotx.at[pl.ds(0, 16)], cotx.at[pl.ds(ROWS, 16)], at_device(device - 1),
        no(first_device), no(last_device), cotx.at[pl.ds(ROWS, 16)],
    )

    load_qg.wait()
    load_kg.wait()
    bias0 = jnp.where(device > 0, 0.0, NEGATIVE_FILL).astype(F32)

    def forward_chunk(chunk, _):
        halo(chunk).wait_recv()
        spans = [pl.ds(multiple(chunk * COLS + k * HEAD, HEAD), HEAD) for k in range(4)]
        results = forward_heads(
            [(n0[:, here], n0p[:, here], qg[0:1, here], kg[0:1, here]) for here in spans], bias0
        )
        for k, (probs, attended) in enumerate(results):
            p0[chunk * 4 + k] = probs
            u0[:, spans[k]] = (tok[:, spans[k]].astype(F32) + attended).astype(BF16)
        h1r[:, cols(chunk)] = (dot(pool_matrix(), u0[:, cols(chunk)]) * 0.25).astype(BF16)
        return 0

    lax.fori_loop(0, 4, forward_chunk, 0)

    h1_rows = h1r[...].astype(F32)
    inv1 = lax.rsqrt(jnp.sum(h1_rows * h1_rows, axis=-1, keepdims=True) / WIDTH + EPSILON)
    n1r[...] = (h1_rows * inv1).astype(BF16)
    n1_copies = to_members(lambda t: n1r.at[:, cols(t)], n1c.at[rows(sub, 32)])
    h1_copies = to_members(lambda t: h1r.at[:, cols(t)], h1.at[rows(sub, 32)])
    n1c[rows(sub, 32), :] = n1r[:, cols(sub)]
    h1[rows(sub, 32), :] = h1r[:, cols(sub)]

    cot_edge.wait_recv()
    row, col = iotas(48, ROWS + 16)
    first = (row < 32) & (col >= 4 * row + 3) & (col <= 4 * row + 6)
    start = 16 * (row - 32) + 15
    second = (row >= 32) & (row < 40) & (col >= start) & (col < start + 16)
    gather = ones_where(first | second)
    for chunk in range(4):
        here = pl.ds(chunk * COLS, COLS)
        summed = dot(gather, cotx[:, here])
        gmr[:, here] = summed[0:32]
        g2r[:, here] = summed[32:40]
    gm_low[...] = gmr[...].astype(BF16)

    arrived(n1_copies)
    n1_next = post_if(n1c, n1p, at_seq(seq + 1), no(last_group), no(first_group), n1p)
    g2_copies = to_members(lambda t: g2r.at[:, cols(t)], g2h.at[rows(sub, 8)])
    gm_copies = to_members(lambda t: gm_low.at[:, cols(t)], gmh.at[rows(sub, 32)])
    g2h[rows(sub, 8), :] = g2r[:, cols(sub)]
    gmh[rows(sub, 32), :] = gm_low[:, cols(sub)]

    bias1 = jnp.where(seq > 0, 0.0, NEGATIVE_FILL).astype(F32)

    def gains(level, k):
        here = pl.ds(multiple(sub * COLS + k * HEAD, HEAD), HEAD)
        return qg[level : level + 1, here], kg[level : level + 1, here]

    n1_next.wait_recv()
    spans = [pl.ds(k * HEAD, HEAD) for k in range(4)]
    results = forward_heads(
        [(n1c[:, here], n1p[:, here], *gains(1, k)) for k, here in enumerate(spans)], bias1
    )
    arrived(h1_copies)
    for k, (probs, attended) in enumerate(results):
        p1[k] = probs
        u1[:, spans[k]] = (h1[:, spans[k]].astype(F32) + attended).astype(BF16)
    h2 = (dot(pool_matrix(), u1[...]) * 0.25).astype(BF16).astype(F32)
    sq[...] = packed(jnp.sum(h2 * h2, axis=-1, keepdims=True))
    sq_copies = [post(sq, sq_in.at[k - 1], (seq, peer(k))) for k in range(1, MEMBERS)]

    def seq_peer(k):
        return lax.rem(in_unit + k, 4)

    arrived(g2_copies)
    gl2[...] = g2h[...].astype(BF16)

    def head_cols(k):
        return pl.ds(multiple(k * HEAD, HEAD), HEAD)

    gl2_copies = [
        post(gl2.at[:, head_cols(seq_peer(k))], gl2h.at[rows(in_unit, 32)], at_seq(unit_base + seq_peer(k)))
        for k in range(1, 4)
    ]
    gl2h[rows(in_unit, 32), :] = gl2[:, head_cols(in_unit)]

    arrived(sq_copies)
    total = unpacked(sq[...] + sq_in[0] + sq_in[1] + sq_in[2])
    inv2 = lax.rsqrt(total / WIDTH + EPSILON)
    n2r[...] = (h2 * inv2).astype(BF16)
    n2_copies = [
        post(n2r.at[:, head_cols(seq_peer(k))], n2c.at[rows(in_unit, 32)], at_seq(unit_base + seq_peer(k)))
        for k in range(1, 4)
    ]
    n2_copies += [
        post_if(
            n2r.at[:, head_cols(seq_peer(k))], n2p.at[rows(in_unit, 32)],
            at_seq(unit_base + 4 + seq_peer(k)),
            no(last_unit), no(first_unit), n2p if k == 0 else None,
        )
        for k in range(4)
    ]
    n2c[rows(in_unit, 32), :] = n2r[:, head_cols(in_unit)]

    u1_copies = to_members(lambda t: u1.at[rows(t, 32)], u1r.at[:, cols(sub)])
    u1r[:, cols(sub)] = u1[rows(sub, 32), :]

    arrived(gl2_copies)
    arrived(n2_copies)
    bias2 = jnp.where(unit_base > 0, 0.0, NEGATIVE_FILL).astype(F32)
    gains2 = gains(2, in_unit)
    ((probs2, attended2),) = forward_heads([(n2c[...], n2p[...], *gains2)], bias2)
    (term_prev,), own_terms2 = backward_heads([(n2c[...], n2p[...], *gains2, probs2, gl2h[...])])
    gp2[...] = term_prev.astype(BF16)
    c2_copies = [
        post_if(
            gp2.at[rows(seq_peer(k), 32)], r2p.at[in_unit], at_seq(unit_base - 4 + seq_peer(k)),
            no(first_unit), no(last_unit), r2p if k == 0 else None,
        )
        for k in range(4)
    ]
    c2[:, 0:HEAD] = attended2.astype(BF16)
    c2[:, HEAD : 2 * HEAD] = own_terms2()[0].astype(BF16)
    c2_copies += [
        post(c2.at[rows(seq_peer(k), 32)], r2c.at[in_unit], at_seq(unit_base + seq_peer(k)))
        for k in range(1, 4)
    ]
    r2c[in_unit] = c2[rows(in_unit, 32), :]

    arrived(c2_copies)
    unit2 = h2 * inv2
    term2 = jnp.concatenate(
        [r2c[k][:, HEAD : 2 * HEAD].astype(F32) + r2p[k].astype(F32) for k in range(4)], axis=1
    )
    dz[...] = packed(jnp.sum(term2 * unit2, axis=-1, keepdims=True))
    dz_copies = [post(dz, dz_in.at[k - 1], (seq, peer(k))) for k in range(1, MEMBERS)]
    attended2_rows = jnp.concatenate([r2c[k][:, 0:HEAD].astype(F32) for k in range(4)], axis=1)
    u2 = (h2 + attended2_rows).astype(BF16)
    u2_wide = u2.astype(F32)
    row, _ = iotas(16, COLS)

    def u1_row(r):
        return u1[r - 15 : r + 1, :].astype(F32)[15:16]

    edge[...] = jnp.where(
        row == 0, u2_wide[31:32], jnp.where(row == 1, u1_row(ROWS - 1), 0.0)
    ).astype(BF16)
    edge_copy = post_if(edge, edge_in, at_seq(seq + 1), no(last_group), no(first_group), edge_in)

    arrived(dz_copies)
    total = unpacked(dz[...] + dz_in[0] + dz_in[1] + dz_in[2])
    back2 = g2h[...] + inv2 * (term2 - unit2 * (total / WIDTH))
    b2[...] = back2
    b2_copies = to_members(lambda t: b2.at[rows(t, 8)], b2r.at[:, cols(sub)])
    b2r[:, cols(sub)] = b2[rows(sub, 8), :]

    arrived(gm_copies)
    grad1 = gmh[...].astype(F32) + split_dot(repeat_matrix(), b2[...]) * 0.25
    gl1[...] = grad1.astype(BF16)
    back_copies = []
    terms_prev, own_terms1 = backward_heads(
        [
            (n1c[:, here], n1p[:, here], *gains(1, k), p1[k], gl1[:, here])
            for k, here in enumerate(spans)
        ]
    )
    for k, term_prev in enumerate(terms_prev):
        gp1[k] = term_prev.astype(BF16)
        back_copies.append(
            post_if(
                gp1.at[k], gr1.at[k], at_seq(seq - 1), no(first_group), no(last_group), gr1.at[k]
            )
        )
    for k, term_cur in enumerate(own_terms1()):
        gc1[:, spans[k]] = term_cur

    edge_copy.wait_recv()
    before = edge_in[...].astype(F32)
    row, _ = iotas(8, COLS)
    for t in range(MEMBERS):
        if t == 0:
            coarse, fine = before[0:1], before[1:2]
        else:
            coarse, fine = u2_wide[8 * t - 1 : 8 * t], u1_row(32 * t - 1)
        tail = jnp.where(row == 0, coarse, jnp.where(row == 1, fine, 0.0))
        u2s[t] = jnp.concatenate([u2_wide[8 * t : 8 * t + 8], tail], axis=0).astype(BF16)
    u2_copies = to_members(lambda t: u2s.at[t], u2r.at[:, cols(sub)])
    u2r[:, cols(sub)] = u2s[sub]

    for k in range(4):
        here = pl.ds(k * HEAD, HEAD)
        back_copies[k].wait_recv()
        g1s[:, here] = (gc1[:, here] + gr1[k].astype(F32)).astype(BF16)
    g1_copies = to_members(lambda t: g1s.at[rows(t, 32)], g1r.at[:, cols(sub)])
    g1r[:, cols(sub)] = g1s[rows(sub, 32), :]

    arrived(b2_copies)
    repeat8 = repeat_matrix()[0:32, 0:8]
    arrived(g1_copies)
    unit1 = h1_rows * inv1
    term1 = g1r[...].astype(F32)
    along = jnp.sum(term1 * unit1, axis=-1, keepdims=True) / WIDTH
    back1 = gmr[...] + split_dot(repeat8, b2r[...]) * 0.25 + inv1 * (term1 - unit1 * along)
    gmr[...] = back1

    back_index = take(4)

    def back_halo(chunk):
        here = cols(chunk)
        copy = remote(gp0.at[:, here], gr0.at[:, here], back_index + chunk, at_device(device - 1))
        return Guarded(copy, no(first_device), no(last_device), gr0.at[:, here])

    def backward_chunk(chunk, _):
        wide = cols(chunk)
        grad = cotx[0:ROWS, wide].astype(F32) + split_dot(repeat_matrix(), gmr[:, wide]) * 0.25
        g0[:, wide] = grad
        spans = [pl.ds(multiple(chunk * COLS + k * HEAD, HEAD), HEAD) for k in range(4)]
        low = grad.astype(BF16)
        terms_prev, own_terms0 = backward_heads(
            [
                (n0[:, here], n0p[:, here], qg[0:1, here], kg[0:1, here],
                 p0[chunk * 4 + k], low[:, k * HEAD : (k + 1) * HEAD])
                for k, here in enumerate(spans)
            ]
        )
        for here, term_prev in zip(spans, terms_prev):
            gp0[:, here] = term_prev.astype(BF16)
        back_halo(chunk).start()
        for here, term_cur in zip(spans, own_terms0()):
            gc0[:, here] = term_cur
        return 0

    lax.fori_loop(0, 4, backward_chunk, 0)

    arrived(u1_copies)
    arrived(u2_copies)
    row, col = iotas(32, 16)
    inside = (col < 8) & (row >= 4 * col + 3) & (row <= 4 * col + 6)
    lift = ones_where(inside | ((col == 8) & (row <= 2) & (device > 0)))

    def output_chunk(chunk, _):
        here = cols(chunk)
        coarse = u2r[:, here]
        mid[0:32, here] = (u1r[:, here].astype(F32) + dot(lift, coarse)).astype(BF16)
        last = coarse.astype(F32)
        last = jnp.where(device > 0, last[8:9] + last[9:10], 0.0)
        mid[32:48, here] = jnp.broadcast_to(last, (16, COLS)).astype(BF16)
        out_v[:, here] = (u0[:, here].astype(F32) + dot(up_matrix(), mid[:, here])).astype(BF16)
        return 0

    lax.fori_loop(0, 4, output_chunk, 0)

    inv = inv0[...]

    def term_chunk(chunk, along):
        here = cols(chunk)
        back_halo(chunk).wait_recv()
        term = gc0[:, here] + gr0[:, here].astype(F32)
        g0[:, here] = g0[:, here] + inv * term
        part = term * tok[:, here].astype(F32)
        return along + sum(part[:, k * HEAD : (k + 1) * HEAD] for k in range(COLS // HEAD))

    along = lax.fori_loop(0, 4, term_chunk, jnp.zeros((ROWS, HEAD), F32))
    weight0[...] = inv * inv * inv * (jnp.sum(along, axis=-1, keepdims=True) / WIDTH)

    def finish_rows(block, _):
        here = pl.ds(multiple(block * 16, 16), 16)
        grad_out[here, :] = (g0[here, :] - weight0[here, :] * tok[here, :].astype(F32)).astype(BF16)
        return 0

    lax.fori_loop(0, ROWS // 16, finish_rows, 0)
    for copy in sent:
        copy.wait_send()
    for chunk in range(4):
        halo(chunk).wait_send()
        back_halo(chunk).wait_send()


def per_device(tokens, cotangent, query_gain, key_gain):
    groups = lax.axis_size("seq")
    shape = jax.ShapeDtypeStruct(tokens.shape, BF16)

    def low(*extent):
        return pltpu.VMEM(extent, BF16)

    def wide(*extent):
        return pltpu.VMEM(extent, F32)

    rows_low = low(ROWS, WIDTH)
    scratch = dict(
        qg=wide(3, WIDTH), kg=wide(3, WIDTH), tok=rows_low, cotx=low(ROWS + 16, WIDTH), n0=rows_low, n0p=rows_low, u0=rows_low,
        p0=wide(HEADS, ROWS, ROWS), inv0=wide(ROWS, 1), weight0=wide(ROWS, 1), gc0=wide(ROWS, WIDTH), gp0=rows_low,
        gr0=rows_low, g0=wide(ROWS, WIDTH),
        h1r=low(32, WIDTH), n1r=low(32, WIDTH), n1c=low(ROWS, COLS), n1p=low(ROWS, COLS),
        h1=low(ROWS, COLS), p1=wide(4, ROWS, ROWS), u1=low(ROWS, COLS), gm_low=low(32, WIDTH),
        gmr=wide(32, WIDTH), g2r=wide(8, WIDTH), gmh=low(ROWS, COLS), g2h=wide(32, COLS),
        sq=wide(8, HEAD), sq_in=wide(3, 8, HEAD), n2r=low(32, COLS), n2c=low(ROWS, HEAD),
        n2p=low(ROWS, HEAD), gl2=low(32, COLS), gl2h=low(ROWS, HEAD), c2=low(ROWS, 2 * HEAD),
        gp2=low(ROWS, HEAD), r2c=low(4, 32, 2 * HEAD), r2p=low(4, 32, HEAD), dz=wide(8, HEAD),
        dz_in=wide(3, 8, HEAD), u1r=low(32, WIDTH), u2s=low(4, 16, COLS), u2r=low(16, WIDTH), mid=low(48, WIDTH), edge=low(16, COLS), edge_in=low(16, COLS),
        b2=wide(32, COLS), b2r=wide(8, WIDTH),
        gl1=low(ROWS, COLS), gc1=wide(ROWS, COLS), gp1=low(4, ROWS, HEAD), gr1=low(4, ROWS, HEAD),
        g1s=low(ROWS, COLS), g1r=low(32, WIDTH),
    )
    hbm = pl.BlockSpec(memory_space=pl.ANY)

    vmem = pl.BlockSpec(memory_space=pltpu.VMEM)

    def body(*refs):
        kernel(groups, *refs)

    return pl.pallas_call(
        body,
        out_shape=(shape, shape),
        in_specs=[hbm] * 4,
        out_specs=(vmem, vmem),
        scratch_shapes=list(scratch.values())
        + [
            pltpu.SemaphoreType.DMA((4,)),
            pltpu.SemaphoreType.DMA((72,)),
            pltpu.SemaphoreType.DMA((72,)),
        ],
        compiler_params=pltpu.CompilerParams(
            collective_id=0, has_side_effects=True, vmem_limit_bytes=int(52.5 * 2**20)
        ),
    )(tokens, cotangent, query_gain, key_gain)


def solution(mesh):
    placed = (P(("seq", "sub"), None), P(("seq", "sub"), None), P(), P())
    return jax.shard_map(
        per_device,
        mesh=mesh,
        in_specs=placed,
        out_specs=(P(("seq", "sub"), None), P(("seq", "sub"), None)),
        check_vma=False,
    )
```

```python
import jax
import jax.numpy as jnp
from jax import lax
from jax.experimental import pallas as pl
from jax.experimental.pallas import tpu as pltpu
from jax.sharding import PartitionSpec as P

HEADS = 16
EPSILON = 1e-06
NEGATIVE_FILL = -1e30
HEAD = 128
ROWS = 128
WIDTH = HEADS * HEAD
MEMBERS = 4
COLS = WIDTH // MEMBERS
MESH = pl.DeviceIdType.MESH
F32 = jnp.float32
BF16 = jnp.bfloat16


def multiple(value, by):
    return pl.multiple_of(value, by)


def iotas(rows, columns):
    shape = (rows, columns)
    return lax.broadcasted_iota(jnp.int32, shape, 0), lax.broadcasted_iota(jnp.int32, shape, 1)


def ones_where(mask):
    return jnp.where(mask, 1.0, 0.0).astype(BF16)


def dot(a, b):
    return lax.dot_general(a, b, (((1,), (0,)), ((), ())), preferred_element_type=F32)


def dot_t(a, b):
    return lax.dot_general(a, b, (((1,), (1,)), ((), ())), preferred_element_type=F32)


def t_dot(a, b):
    return lax.dot_general(a, b, (((0,), (0,)), ((), ())), preferred_element_type=F32)


def split_dot(ones, x):
    high = x.astype(BF16)
    low = (x - high.astype(F32)).astype(BF16)
    return dot(ones, high) + dot(ones, low)


def own_mask():
    query, key = iotas(ROWS, ROWS)
    return key <= query


def gained(normed, gain):
    return (normed.astype(F32) * gain).astype(BF16)


def forward_heads(heads, prev_bias):
    own = own_mask()
    scale = HEAD ** (-0.5)
    queries = [gained(cur, qg) for cur, _, qg, _ in heads]
    near = [dot_t(q, gained(h[0], h[3])) for q, h in zip(queries, heads)]
    far = [dot_t(q, gained(h[1], h[3])) for q, h in zip(queries, heads)]
    scores = [jnp.where(own, a * scale, b * scale + prev_bias) for a, b in zip(near, far)]
    tops = [jnp.max(s, axis=-1, keepdims=True) for s in scores]
    weights = [jnp.exp(s - t) for s, t in zip(scores, tops)]
    sums = [jnp.sum(w, axis=-1, keepdims=True) for w in weights]
    probs = [w / s for w, s in zip(weights, sums)]
    low = [p.astype(BF16) for p in probs]
    zero = jnp.zeros((ROWS, ROWS), BF16)
    attended = [
        dot(jnp.where(own, p, zero), h[0]) + dot(jnp.where(own, zero, p), h[1])
        for p, h in zip(low, heads)
    ]
    return list(zip(probs, attended))


def backward_heads(heads):
    own = own_mask()
    zero = jnp.zeros((ROWS, ROWS), BF16)
    queries = [gained(h[0], h[2]) for h in heads]
    d_probs = [jnp.where(own, dot_t(h[5], h[0]), dot_t(h[5], h[1])) for h in heads]
    low = [h[4].astype(BF16) for h in heads]
    v_prev = [t_dot(jnp.where(own, zero, p), h[5]) for p, h in zip(low, heads)]
    centers = [jnp.sum(h[4] * d, axis=-1, keepdims=True) for h, d in zip(heads, d_probs)]
    d_scores = [
        (h[4] * (d - c) * HEAD ** (-0.5)).astype(BF16) for h, d, c in zip(heads, d_probs, centers)
    ]
    ds_cur = [jnp.where(own, d, zero) for d in d_scores]
    ds_prev = [jnp.where(own, zero, d) for d in d_scores]
    k_prev = [t_dot(d, q) for d, q in zip(ds_prev, queries)]
    terms_prev = [kp * h[3] + vp for h, kp, vp in zip(heads, k_prev, v_prev)]

    def own_terms():
        v_cur = [t_dot(jnp.where(own, p, zero), h[5]) for p, h in zip(low, heads)]
        k_cur = [t_dot(d, q) for d, q in zip(ds_cur, queries)]
        d_query = [
            dot(a, gained(h[0], h[3])) + dot(b, gained(h[1], h[3]))
            for a, b, h in zip(ds_cur, ds_prev, heads)
        ]
        return [
            dq * h[2] + kc * h[3] + vc for h, dq, kc, vc in zip(heads, d_query, k_cur, v_cur)
        ]

    return terms_prev, own_terms


def packed(column):
    row, col = iotas(32, HEAD)
    line = jnp.sum(jnp.where(row == col, column, 0.0), axis=0, keepdims=True)
    return jnp.broadcast_to(line, (8, HEAD))


def unpacked(tile):
    row, col = iotas(32, HEAD)
    line = jnp.broadcast_to(tile[0:1], (32, HEAD))
    return jnp.sum(jnp.where(row == col, line, 0.0), axis=-1, keepdims=True)


def up_matrix():
    row, col = iotas(ROWS, 48)
    inside = (col < 32) & (row >= 4 * col + 3) & (row <= 4 * col + 6)
    return ones_where(inside | ((col == 32) & (row <= 2)))


def repeat_matrix():
    row, col = iotas(ROWS, 32)
    return ones_where((row >= 4 * col) & (row < 4 * col + 4))


def pool_matrix():
    row, col = iotas(32, ROWS)
    return ones_where((col >= 4 * row) & (col < 4 * row + 4))


class Guarded:
    def __init__(self, copy, sends, takes, blank=None):
        self.copy, self.sends, self.takes, self.blank = copy, sends, takes, blank

    def start(self):
        @pl.when(self.sends)
        def _():
            self.copy.start()

    def wait_recv(self):
        @pl.when(self.takes)
        def _():
            self.copy.wait_recv()

        if self.blank is not None:

            @pl.when(jnp.logical_not(self.takes))
            def _():
                self.blank[...] = jnp.zeros(self.blank.shape, self.blank.dtype)

    def wait_send(self):
        @pl.when(self.sends)
        def _():
            self.copy.wait_send()


def kernel(
    groups, tokens_hbm, cot_hbm, qg_hbm, kg_hbm, out_v, grad_out,
    qg, kg, tok, cotx, n0, n0p, u0, p0, inv0, weight0, gc0, gp0, gr0, g0,
    h1r, n1r, n1c, n1p, h1, p1, u1, gm_low, gmr, g2r, gmh, g2h,
    sq, sq_in, n2r, n2c, n2p, gl2, gl2h, c2, gp2, r2c, r2p, dz, dz_in,
    u1r, u2s, u2r, mid, edge, edge_in, b2, b2r, gl1, gc1, gp1, gr1, g1s, g1r,
    local_sem, send_sem, recv_sem,
):
    seq = lax.axis_index("seq")
    sub = lax.axis_index("sub")
    devices = groups * MEMBERS
    device = seq * MEMBERS + sub
    in_unit = lax.rem(seq, 4)
    unit_base = seq - in_unit

    first_device, last_device = device == 0, device == devices - 1
    first_group, last_group = seq == 0, seq == groups - 1
    first_unit, last_unit = unit_base == 0, unit_base == groups - 4
    no = jnp.logical_not

    def at_seq(s):
        return (lax.rem(s + groups, groups), sub)

    def at_device(d):
        d = lax.rem(d + devices, devices)
        return (lax.div(d, MEMBERS), lax.rem(d, MEMBERS))

    def peer(k):
        return lax.rem(sub + k, MEMBERS)

    used = [0]
    sent = []

    def take(count):
        used[0] += count
        return used[0] - count

    def remote(src, dst, index, target):
        return pltpu.make_async_remote_copy(
            src_ref=src, dst_ref=dst, send_sem=send_sem.at[index], recv_sem=recv_sem.at[index],
            device_id=target, device_id_type=MESH,
        )

    def post(src, dst, target):
        copy = remote(src, dst, take(1), target)
        copy.start()
        sent.append(copy)
        return copy

    def post_if(src, dst, target, sends, takes, blank=None):
        copy = Guarded(remote(src, dst, take(1), target), sends, takes, blank)
        copy.start()
        sent.append(copy)
        return copy

    def to_members(source, target_ref):
        return [post(source(peer(k)), target_ref, (seq, peer(k))) for k in range(1, MEMBERS)]

    def arrived(copies):
        for copy in copies:
            copy.wait_recv()

    def cols(member):
        return pl.ds(multiple(member * COLS, COLS), COLS)

    def rows(index, count):
        return pl.ds(multiple(index * count, count), count)

    load_tok = pltpu.make_async_copy(tokens_hbm, tok, local_sem.at[0])
    load_cot = pltpu.make_async_copy(cot_hbm, cotx.at[pl.ds(0, ROWS)], local_sem.at[1])
    load_qg = pltpu.make_async_copy(qg_hbm, qg, local_sem.at[2])
    load_kg = pltpu.make_async_copy(kg_hbm, kg, local_sem.at[3])
    load_tok.start()
    load_qg.start()
    load_kg.start()
    load_cot.start()
    barrier = pltpu.get_barrier_semaphore()
    partners = [(at_device(device + 1), no(last_device)), (at_device(device - 1), no(first_device))]
    partners += [((seq, peer(k)), None) for k in range(1, MEMBERS)]
    partners += [(at_seq(unit_base + lax.rem(in_unit + k, 4)), None) for k in range(1, 4)]
    partners += [(at_seq(unit_base + 4 + k), no(last_unit)) for k in range(4)]
    partners += [(at_seq(unit_base - 4 + k), no(first_unit)) for k in range(4)]
    expected = 0
    for partner, present in partners:

        def greet(partner=partner):
            pl.semaphore_signal(barrier, inc=1, device_id=partner, device_id_type=MESH)

        if present is None:
            greet()
            expected = expected + 1
        else:
            pl.when(present)(greet)
            expected = expected + jnp.where(present, 1, 0)

    load_tok.wait()

    def normalize_rows(block, _):
        here = pl.ds(multiple(block * 16, 16), 16)
        x = tok[here, :].astype(F32)
        inv = lax.rsqrt(jnp.sum(x * x, axis=-1, keepdims=True) / WIDTH + EPSILON)
        inv0[here, :] = inv
        n0[here, :] = (x * inv).astype(BF16)
        return 0

    lax.fori_loop(0, ROWS // 16, normalize_rows, 0)
    pl.semaphore_wait(barrier, expected)

    halo_index = take(4)

    def halo(chunk):
        here = cols(chunk)
        copy = remote(n0.at[:, here], n0p.at[:, here], halo_index + chunk, at_device(device + 1))
        return Guarded(copy, no(last_device), no(first_device), n0p.at[:, here])

    for chunk in range(4):
        halo(chunk).start()
    load_cot.wait()
    cot_edge = post_if(
        cotx.at[pl.ds(0, 16)], cotx.at[pl.ds(ROWS, 16)], at_device(device - 1),
        no(first_device), no(last_device), cotx.at[pl.ds(ROWS, 16)],
    )

    load_qg.wait()
    load_kg.wait()
    bias0 = jnp.where(device > 0, 0.0, NEGATIVE_FILL).astype(F32)

    def forward_chunk(chunk, _):
        halo(chunk).wait_recv()
        spans = [pl.ds(multiple(chunk * COLS + k * HEAD, HEAD), HEAD) for k in range(4)]
        results = forward_heads(
            [(n0[:, here], n0p[:, here], qg[0:1, here], kg[0:1, here]) for here in spans], bias0
        )
        for k, (probs, attended) in enumerate(results):
            p0[chunk * 4 + k] = probs
            u0[:, spans[k]] = (tok[:, spans[k]].astype(F32) + attended).astype(BF16)
        h1r[:, cols(chunk)] = (dot(pool_matrix(), u0[:, cols(chunk)]) * 0.25).astype(BF16)
        return 0

    lax.fori_loop(0, 4, forward_chunk, 0)

    h1_rows = h1r[...].astype(F32)
    inv1 = lax.rsqrt(jnp.sum(h1_rows * h1_rows, axis=-1, keepdims=True) / WIDTH + EPSILON)
    n1r[...] = (h1_rows * inv1).astype(BF16)
    n1_copies = to_members(lambda t: n1r.at[:, cols(t)], n1c.at[rows(sub, 32)])
    h1_copies = to_members(lambda t: h1r.at[:, cols(t)], h1.at[rows(sub, 32)])
    n1c[rows(sub, 32), :] = n1r[:, cols(sub)]
    h1[rows(sub, 32), :] = h1r[:, cols(sub)]

    cot_edge.wait_recv()
    row, col = iotas(48, ROWS + 16)
    first = (row < 32) & (col >= 4 * row + 3) & (col <= 4 * row + 6)
    start = 16 * (row - 32) + 15
    second = (row >= 32) & (row < 40) & (col >= start) & (col < start + 16)
    gather = ones_where(first | second)
    for chunk in range(4):
        here = pl.ds(chunk * COLS, COLS)
        summed = dot(gather, cotx[:, here])
        gmr[:, here] = summed[0:32]
        g2r[:, here] = summed[32:40]
    gm_low[...] = gmr[...].astype(BF16)

    arrived(n1_copies)
    n1_next = post_if(n1c, n1p, at_seq(seq + 1), no(last_group), no(first_group), n1p)
    g2_copies = to_members(lambda t: g2r.at[:, cols(t)], g2h.at[rows(sub, 8)])
    g2h[rows(sub, 8), :] = g2r[:, cols(sub)]
    gmh[rows(sub, 32), :] = gm_low[:, cols(sub)]

    bias1 = jnp.where(seq > 0, 0.0, NEGATIVE_FILL).astype(F32)

    def gains(level, k):
        here = pl.ds(multiple(sub * COLS + k * HEAD, HEAD), HEAD)
        return qg[level : level + 1, here], kg[level : level + 1, here]

    n1_next.wait_recv()
    spans = [pl.ds(k * HEAD, HEAD) for k in range(4)]
    results = forward_heads(
        [(n1c[:, here], n1p[:, here], *gains(1, k)) for k, here in enumerate(spans)], bias1
    )
    arrived(h1_copies)
    for k, (probs, attended) in enumerate(results):
        p1[k] = probs
        u1[:, spans[k]] = (h1[:, spans[k]].astype(F32) + attended).astype(BF16)
    h2 = (dot(pool_matrix(), u1[...]) * 0.25).astype(BF16).astype(F32)
    sq[...] = packed(jnp.sum(h2 * h2, axis=-1, keepdims=True))
    sq_copies = [post(sq, sq_in.at[k - 1], (seq, peer(k))) for k in range(1, MEMBERS)]

    def seq_peer(k):
        return lax.rem(in_unit + k, 4)

    arrived(g2_copies)
    gl2[...] = g2h[...].astype(BF16)

    def head_cols(k):
        return pl.ds(multiple(k * HEAD, HEAD), HEAD)

    gl2_copies = [
        post(gl2.at[:, head_cols(seq_peer(k))], gl2h.at[rows(in_unit, 32)], at_seq(unit_base + seq_peer(k)))
        for k in range(1, 4)
    ]
    gl2h[rows(in_unit, 32), :] = gl2[:, head_cols(in_unit)]

    arrived(sq_copies)
    total = unpacked(sq[...] + sq_in[0] + sq_in[1] + sq_in[2])
    inv2 = lax.rsqrt(total / WIDTH + EPSILON)
    n2r[...] = (h2 * inv2).astype(BF16)
    n2_copies = [
        post(n2r.at[:, head_cols(seq_peer(k))], n2c.at[rows(in_unit, 32)], at_seq(unit_base + seq_peer(k)))
        for k in range(1, 4)
    ]
    n2_copies += [
        post_if(
            n2r.at[:, head_cols(seq_peer(k))], n2p.at[rows(in_unit, 32)],
            at_seq(unit_base + 4 + seq_peer(k)),
            no(last_unit), no(first_unit), n2p if k == 0 else None,
        )
        for k in range(4)
    ]
    n2c[rows(in_unit, 32), :] = n2r[:, head_cols(in_unit)]

    gm_copies = to_members(lambda t: gm_low.at[:, cols(t)], gmh.at[rows(sub, 32)])
    u1_copies = to_members(lambda t: u1.at[rows(t, 32)], u1r.at[:, cols(sub)])
    u1r[:, cols(sub)] = u1[rows(sub, 32), :]

    arrived(gl2_copies)
    arrived(n2_copies)
    bias2 = jnp.where(unit_base > 0, 0.0, NEGATIVE_FILL).astype(F32)
    gains2 = gains(2, in_unit)
    ((probs2, attended2),) = forward_heads([(n2c[...], n2p[...], *gains2)], bias2)
    (term_prev,), own_terms2 = backward_heads([(n2c[...], n2p[...], *gains2, probs2, gl2h[...])])
    gp2[...] = term_prev.astype(BF16)
    c2_copies = [
        post_if(
            gp2.at[rows(seq_peer(k), 32)], r2p.at[in_unit], at_seq(unit_base - 4 + seq_peer(k)),
            no(first_unit), no(last_unit), r2p if k == 0 else None,
        )
        for k in range(4)
    ]
    c2[:, 0:HEAD] = attended2.astype(BF16)
    c2[:, HEAD : 2 * HEAD] = own_terms2()[0].astype(BF16)
    c2_copies += [
        post(c2.at[rows(seq_peer(k), 32)], r2c.at[in_unit], at_seq(unit_base + seq_peer(k)))
        for k in range(1, 4)
    ]
    r2c[in_unit] = c2[rows(in_unit, 32), :]

    arrived(c2_copies)
    unit2 = h2 * inv2
    term2 = jnp.concatenate(
        [r2c[k][:, HEAD : 2 * HEAD].astype(F32) + r2p[k].astype(F32) for k in range(4)], axis=1
    )
    dz[...] = packed(jnp.sum(term2 * unit2, axis=-1, keepdims=True))
    dz_copies = [post(dz, dz_in.at[k - 1], (seq, peer(k))) for k in range(1, MEMBERS)]
    attended2_rows = jnp.concatenate([r2c[k][:, 0:HEAD].astype(F32) for k in range(4)], axis=1)
    u2 = (h2 + attended2_rows).astype(BF16)
    u2_wide = u2.astype(F32)
    row, _ = iotas(16, COLS)

    def u1_row(r):
        return u1[r - 15 : r + 1, :].astype(F32)[15:16]

    edge[...] = jnp.where(
        row == 0, u2_wide[31:32], jnp.where(row == 1, u1_row(ROWS - 1), 0.0)
    ).astype(BF16)
    edge_copy = post_if(edge, edge_in, at_seq(seq + 1), no(last_group), no(first_group), edge_in)

    arrived(dz_copies)
    total = unpacked(dz[...] + dz_in[0] + dz_in[1] + dz_in[2])
    back2 = g2h[...] + inv2 * (term2 - unit2 * (total / WIDTH))
    b2[...] = back2
    b2_copies = to_members(lambda t: b2.at[rows(t, 8)], b2r.at[:, cols(sub)])
    b2r[:, cols(sub)] = b2[rows(sub, 8), :]

    arrived(gm_copies)
    grad1 = gmh[...].astype(F32) + split_dot(repeat_matrix(), b2[...]) * 0.25
    gl1[...] = grad1.astype(BF16)
    back_copies = []
    terms_prev, own_terms1 = backward_heads(
        [
            (n1c[:, here], n1p[:, here], *gains(1, k), p1[k], gl1[:, here])
            for k, here in enumerate(spans)
        ]
    )
    for k, term_prev in enumerate(terms_prev):
        gp1[k] = term_prev.astype(BF16)
        back_copies.append(
            post_if(
                gp1.at[k], gr1.at[k], at_seq(seq - 1), no(first_group), no(last_group), gr1.at[k]
            )
        )
    for k, term_cur in enumerate(own_terms1()):
        gc1[:, spans[k]] = term_cur

    edge_copy.wait_recv()
    before = edge_in[...].astype(F32)
    row, _ = iotas(8, COLS)
    for t in range(MEMBERS):
        if t == 0:
            coarse, fine = before[0:1], before[1:2]
        else:
            coarse, fine = u2_wide[8 * t - 1 : 8 * t], u1_row(32 * t - 1)
        tail = jnp.where(row == 0, coarse, jnp.where(row == 1, fine, 0.0))
        u2s[t] = jnp.concatenate([u2_wide[8 * t : 8 * t + 8], tail], axis=0).astype(BF16)
    u2_copies = to_members(lambda t: u2s.at[t], u2r.at[:, cols(sub)])
    u2r[:, cols(sub)] = u2s[sub]

    for k in range(4):
        here = pl.ds(k * HEAD, HEAD)
        back_copies[k].wait_recv()
        g1s[:, here] = (gc1[:, here] + gr1[k].astype(F32)).astype(BF16)
    g1_copies = to_members(lambda t: g1s.at[rows(t, 32)], g1r.at[:, cols(sub)])
    g1r[:, cols(sub)] = g1s[rows(sub, 32), :]

    arrived(b2_copies)
    repeat8 = repeat_matrix()[0:32, 0:8]
    arrived(g1_copies)
    unit1 = h1_rows * inv1
    term1 = g1r[...].astype(F32)
    along = jnp.sum(term1 * unit1, axis=-1, keepdims=True) / WIDTH
    back1 = gmr[...] + split_dot(repeat8, b2r[...]) * 0.25 + inv1 * (term1 - unit1 * along)
    gmr[...] = back1

    back_index = take(4)

    def back_halo(chunk):
        here = cols(chunk)
        copy = remote(gp0.at[:, here], gr0.at[:, here], back_index + chunk, at_device(device - 1))
        return Guarded(copy, no(first_device), no(last_device), gr0.at[:, here])

    def backward_chunk(chunk, _):
        wide = cols(chunk)
        grad = cotx[0:ROWS, wide].astype(F32) + split_dot(repeat_matrix(), gmr[:, wide]) * 0.25
        g0[:, wide] = grad
        spans = [pl.ds(multiple(chunk * COLS + k * HEAD, HEAD), HEAD) for k in range(4)]
        low = grad.astype(BF16)
        terms_prev, own_terms0 = backward_heads(
            [
                (n0[:, here], n0p[:, here], qg[0:1, here], kg[0:1, here],
                 p0[chunk * 4 + k], low[:, k * HEAD : (k + 1) * HEAD])
                for k, here in enumerate(spans)
            ]
        )
        for here, term_prev in zip(spans, terms_prev):
            gp0[:, here] = term_prev.astype(BF16)
        back_halo(chunk).start()
        for here, term_cur in zip(spans, own_terms0()):
            gc0[:, here] = term_cur
        return 0

    lax.fori_loop(0, 4, backward_chunk, 0)

    arrived(u1_copies)
    arrived(u2_copies)
    row, col = iotas(32, 16)
    inside = (col < 8) & (row >= 4 * col + 3) & (row <= 4 * col + 6)
    lift = ones_where(inside | ((col == 8) & (row <= 2) & (device > 0)))

    def output_chunk(chunk, _):
        here = cols(chunk)
        coarse = u2r[:, here]
        mid[0:32, here] = (u1r[:, here].astype(F32) + dot(lift, coarse)).astype(BF16)
        last = coarse.astype(F32)
        last = jnp.where(device > 0, last[8:9] + last[9:10], 0.0)
        mid[32:48, here] = jnp.broadcast_to(last, (16, COLS)).astype(BF16)
        out_v[:, here] = (u0[:, here].astype(F32) + dot(up_matrix(), mid[:, here])).astype(BF16)
        return 0

    lax.fori_loop(0, 4, output_chunk, 0)

    inv = inv0[...]

    def term_chunk(chunk, along):
        here = cols(chunk)
        back_halo(chunk).wait_recv()
        term = gc0[:, here] + gr0[:, here].astype(F32)
        g0[:, here] = g0[:, here] + inv * term
        part = term * tok[:, here].astype(F32)
        return along + sum(part[:, k * HEAD : (k + 1) * HEAD] for k in range(COLS // HEAD))

    along = lax.fori_loop(0, 4, term_chunk, jnp.zeros((ROWS, HEAD), F32))
    weight0[...] = inv * inv * inv * (jnp.sum(along, axis=-1, keepdims=True) / WIDTH)

    def finish_rows(block, _):
        here = pl.ds(multiple(block * 16, 16), 16)
        grad_out[here, :] = (g0[here, :] - weight0[here, :] * tok[here, :].astype(F32)).astype(BF16)
        return 0

    lax.fori_loop(0, ROWS // 16, finish_rows, 0)
    for copy in sent:
        copy.wait_send()
    for chunk in range(4):
        halo(chunk).wait_send()
        back_halo(chunk).wait_send()


def per_device(tokens, cotangent, query_gain, key_gain):
    groups = lax.axis_size("seq")
    shape = jax.ShapeDtypeStruct(tokens.shape, BF16)

    def low(*extent):
        return pltpu.VMEM(extent, BF16)

    def wide(*extent):
        return pltpu.VMEM(extent, F32)

    rows_low = low(ROWS, WIDTH)
    scratch = dict(
        qg=wide(3, WIDTH), kg=wide(3, WIDTH), tok=rows_low, cotx=low(ROWS + 16, WIDTH), n0=rows_low, n0p=rows_low, u0=rows_low,
        p0=wide(HEADS, ROWS, ROWS), inv0=wide(ROWS, 1), weight0=wide(ROWS, 1), gc0=wide(ROWS, WIDTH), gp0=rows_low,
        gr0=rows_low, g0=wide(ROWS, WIDTH),
        h1r=low(32, WIDTH), n1r=low(32, WIDTH), n1c=low(ROWS, COLS), n1p=low(ROWS, COLS),
        h1=low(ROWS, COLS), p1=wide(4, ROWS, ROWS), u1=low(ROWS, COLS), gm_low=low(32, WIDTH),
        gmr=wide(32, WIDTH), g2r=wide(8, WIDTH), gmh=low(ROWS, COLS), g2h=wide(32, COLS),
        sq=wide(8, HEAD), sq_in=wide(3, 8, HEAD), n2r=low(32, COLS), n2c=low(ROWS, HEAD),
        n2p=low(ROWS, HEAD), gl2=low(32, COLS), gl2h=low(ROWS, HEAD), c2=low(ROWS, 2 * HEAD),
        gp2=low(ROWS, HEAD), r2c=low(4, 32, 2 * HEAD), r2p=low(4, 32, HEAD), dz=wide(8, HEAD),
        dz_in=wide(3, 8, HEAD), u1r=low(32, WIDTH), u2s=low(4, 16, COLS), u2r=low(16, WIDTH), mid=low(48, WIDTH), edge=low(16, COLS), edge_in=low(16, COLS),
        b2=wide(32, COLS), b2r=wide(8, WIDTH),
        gl1=low(ROWS, COLS), gc1=wide(ROWS, COLS), gp1=low(4, ROWS, HEAD), gr1=low(4, ROWS, HEAD),
        g1s=low(ROWS, COLS), g1r=low(32, WIDTH),
    )
    hbm = pl.BlockSpec(memory_space=pl.ANY)

    vmem = pl.BlockSpec(memory_space=pltpu.VMEM)

    def body(*refs):
        kernel(groups, *refs)

    return pl.pallas_call(
        body,
        out_shape=(shape, shape),
        in_specs=[hbm] * 4,
        out_specs=(vmem, vmem),
        scratch_shapes=list(scratch.values())
        + [
            pltpu.SemaphoreType.DMA((4,)),
            pltpu.SemaphoreType.DMA((72,)),
            pltpu.SemaphoreType.DMA((72,)),
        ],
        compiler_params=pltpu.CompilerParams(
            collective_id=0, has_side_effects=True, vmem_limit_bytes=int(52.5 * 2**20)
        ),
    )(tokens, cotangent, query_gain, key_gain)


def solution(mesh):
    placed = (P(("seq", "sub"), None), P(("seq", "sub"), None), P(), P())
    return jax.shard_map(
        per_device,
        mesh=mesh,
        in_specs=placed,
        out_specs=(P(("seq", "sub"), None), P(("seq", "sub"), None)),
        check_vma=False,
    )
```
